32 devices in a mesh: row: 4 (over x, core), col: 4 (over z), win: 2 (over y).
Axes of the slice: x: 2, y: 2, z: 4, core: 2. Of those that a mesh axis runs over, the one named last changes fastest.
Arguments:
- spectra: float32 [2, 2, 16, 2, 16384], P('win', None, ('row', 'col')), may hold values from -8 to 8
- tile_rows: int32 [8256], P(('row', 'col')), may hold values from 0 to 127, as said below
- tile_cols: int32 [8256], P(('row', 'col')), may hold values from 0 to 127, as said below
Outputs:
- cross: float32 [8256, 2, 2, 128, 128], P(('row', 'col'), None, None, 'win')
The draws below stay inside these ranges and needn't reach their ends.
Inputs may be any that keep to these rules, and one draw needn't show every extreme that they name: tile_rows[k] <= tile_cols[k] for every k, and the pairs (tile_rows[k], tile_cols[k]) are all pairs of channel blocks with row block at most column block, each exactly once, in an order drawn from the seed. `tile_cols`: see tile_rows.
All inputs are finite; a program needn't handle non-finite values.
Results may differ from the reference program's by a relative error of at most 0.006.
Values may be sent and summed in bfloat16 or wider, within the bound.
No kernel may reach another device: no remote copies, remote signals or barrier semaphores. Data moves between devices by JAX's collectives and lax.ppermute only.
A program may use at most 320 MiB of HBM per device.

```python
import jax
import jax.numpy as jnp
from jax import lax

CHANNELS = 16384
BLOCK = 128
FREQS = 2
BLOCKS = 128
GROUPS = 2
WIN_GROUP = 16
WINDOWS = 32
PAIR_TILES = 8256
TILES_DEV = 516


def tile_pairs(key):
    first, second = jnp.triu_indices(BLOCKS)
    shuffle = jax.random.permutation(jax.random.fold_in(key, 7), first.shape[0])
    return (first[shuffle].astype(jnp.int32), second[shuffle].astype(jnp.int32))


def draw_tile_rows(key, part):
    return tile_pairs(key)[0]


def draw_tile_cols(key, part):
    return tile_pairs(key)[1]


def levels(key, extent, pieces, low, high):
    def one(axis_at, blocks):
        draws = jax.random.uniform(jax.random.fold_in(jax.random.fold_in(key, 6), axis_at), (blocks,), jnp.float32, low / len(pieces), high / len(pieces))
        return jnp.repeat(jnp.exp(draws), extent[axis_at] // blocks).reshape((-1,) + (1,) * (len(extent) - axis_at - 1))

    factor_of = one(*pieces[0])
    for cut in pieces[1:]:
        factor_of = factor_of * one(*cut)
    return factor_of


def centred(stream_key, shape, scale, limit, cuts=(), kind=jnp.bfloat16):
    values = jax.random.normal(stream_key, shape, jnp.float32) * scale
    if len(cuts) > 0:
        values = levels(stream_key, shape, cuts, -0.22, 0.18) * values
    return jnp.clip(values, min=-limit, max=limit).astype(kind)


def setup_inputs(seed: int = 0) -> dict:
    streams_of = jax.random.split(jax.random.key(seed), 4)
    return {
        "spectra": centred(streams_of[0], (GROUPS, FREQS, WIN_GROUP, 2, CHANNELS), 1.5, 8.0, ((0, 2), (2, 16)), jnp.float32),
        "tile_rows": draw_tile_rows(jax.random.fold_in(streams_of[3], 71), 0),
        "tile_cols": draw_tile_cols(jax.random.fold_in(streams_of[3], 71), 0),
    }


def whiten(spectra):
    power_sum = lax.optimization_barrier(jnp.sum(spectra * spectra, axis=(1, 3), keepdims=True)) / spectra.shape[1]
    return (spectra / jnp.maximum(jnp.sqrt(power_sum), 1.0)).astype(jnp.bfloat16)

def reference(spectra, tile_rows, tile_cols):
    whitened = whiten(spectra).astype(jnp.float32)
    blocks = whitened.reshape(GROUPS, FREQS, WIN_GROUP, 2, BLOCKS, BLOCK)
    norm_scale = 1.0 / jnp.sqrt(jnp.float32(WINDOWS))
    row_batches = tile_rows.reshape(-1, TILES_DEV)
    col_batches = tile_cols.reshape(-1, TILES_DEV)

    def tile_batch(pair):
        left_block = jnp.take(blocks, pair[0], axis=4)
        right_block = jnp.take(blocks, pair[1], axis=4)
        real_part = jnp.einsum('gfwpka,gfwpkb->gkfab', left_block, right_block)
        imag_part = jnp.einsum('gfwka,gfwkb->gkfab', left_block[:, :, :, 0], right_block[:, :, :, 1])
        imag_part = imag_part - jnp.einsum('gfwka,gfwkb->gkfab', left_block[:, :, :, 1], right_block[:, :, :, 0])
        partial_value = jnp.stack([real_part, imag_part], axis=3) * norm_scale
        rounded = lax.optimization_barrier(partial_value.astype(jnp.bfloat16))
        return lax.optimization_barrier(jnp.sum(rounded.astype(jnp.float32), axis=0))
    stacked = lax.map(tile_batch, (row_batches, col_batches))
    return stacked.reshape(PAIR_TILES, FREQS, 2, BLOCK, BLOCK)
```

```python
import functools

import jax
import jax.numpy as jnp
from jax import lax
from jax.experimental import pallas as pl
from jax.experimental.pallas import tpu as pltpu
from jax.sharding import PartitionSpec as P

BLOCK = 128


def whiten_kernel(spectra_ref, *out_refs):
    freqs = spectra_ref.shape[0]
    power = None
    for freq in range(freqs):
        slab = spectra_ref[freq]
        term = jnp.sum(slab * slab, axis=1, keepdims=True)
        power = term if power is None else power + term
    floor = jnp.maximum(jnp.sqrt(power / freqs), 1.0)
    for freq in range(freqs):
        out_refs[freq][...] = (spectra_ref[freq] / floor).astype(jnp.bfloat16)


def whiten(spectra):
    freqs, windows, parts, channels = spectra.shape
    shape = jax.ShapeDtypeStruct((windows, parts, channels), jnp.bfloat16)
    slabs = pl.pallas_call(whiten_kernel, out_shape=[shape] * freqs, name="whiten")(spectra)
    return [slab.reshape(windows * parts, channels) for slab in slabs]


def shift(value, axis, step, inner=1):
    size = lax.axis_size(axis)
    stops = size // inner
    perm = [(at, (at // inner + step) % stops * inner + at % inner) for at in range(size)]
    return lax.ppermute(value, axis, perm)


def gather_windows(own):
    row_size = lax.axis_size("row")
    cores = 2 if row_size % 2 == 0 else 1
    line = [own] + [shift(own, "col", step) for step in range(1, lax.axis_size("col"))]
    block = jnp.concatenate(line, axis=0)
    half = block.shape[1] // 2
    along_row = [shift(block, "row", step, cores) for step in range(1, row_size // cores)]
    along_win = [shift(block, "win", step) for step in range(1, lax.axis_size("win"))]
    whole = [block] + along_row + along_win
    split = []
    for row_step, from_row in enumerate(along_row, 1):
        for win_step, from_win in enumerate(along_win, 1):
            low = shift(from_win[:, :half], "row", row_step, cores)
            high = shift(from_row[:, half:], "win", win_step)
            split.append((low, high))
    if cores == 2:
        swap = functools.partial(
            lax.ppermute, axis_name="row", perm=[(at, at ^ 1) for at in range(row_size)]
        )
        whole = whole + [swap(value) for value in whole]
        split = split + [(swap(low), swap(high)) for low, high in split]
    return whole, split


def stack_kernel(
    counts, parts_rows, scale, rows_ref, cols_ref, *refs
):
    whole_count, split_count, aliased = counts
    whole = refs[:whole_count]
    low = refs[whole_count : whole_count + split_count]
    high = refs[whole_count + split_count : whole_count + 2 * split_count]
    out_ref, left_ref, right_ref = refs[whole_count + 2 * split_count + aliased :]
    depth = left_ref.shape[1]
    row_count = out_ref.shape[3]
    tiles = out_ref.shape[0]
    step = pl.program_id(0)

    @pl.when(step == 0)
    def _():
        offset = lax.axis_index("win") * row_count
        pick_at = lax.broadcasted_iota(jnp.int32, (2 * row_count, 2 * BLOCK), 0)
        pick_lane = lax.broadcasted_iota(jnp.int32, (2 * row_count, 2 * BLOCK), 1)
        want = pick_at % row_count + offset + pick_at // row_count * BLOCK
        pick = (pick_lane == want).astype(jnp.bfloat16)
        turn_at = lax.broadcasted_iota(jnp.int32, (depth, depth), 0)
        turn_lane = lax.broadcasted_iota(jnp.int32, (depth, depth), 1)
        is_imag = turn_at % 2 == 1
        turn = jnp.where(
            is_imag,
            jnp.where(turn_lane == turn_at - 1, -1.0, 0.0),
            jnp.where(turn_lane == turn_at + 1, 1.0, 0.0),
        ).astype(jnp.bfloat16)

        def prepare(halves, first):
            pairs = halves[0].shape[1] // (2 * BLOCK) if halves else whole[0].shape[1] // (4 * BLOCK)

            def body(at, carry):
                here = pl.multiple_of((at + first) * 2 * BLOCK, 2 * BLOCK)
                near = pl.multiple_of(at * 2 * BLOCK, 2 * BLOCK)
                pieces = [ref[:, pl.ds(here, 2 * BLOCK)] for ref in whole]
                pieces += [ref[:, pl.ds(near, 2 * BLOCK)] for ref in halves]
                rows = jnp.concatenate(pieces, axis=0)
                turned = jnp.dot(turn, rows, preferred_element_type=jnp.float32)
                turned = turned.astype(jnp.bfloat16)
                left = lax.dot_general(
                    pick, rows, (((1,), (1,)), ((), ())), preferred_element_type=jnp.float32
                )
                where = pl.multiple_of((at + first) * 2 * row_count, 2 * row_count)
                left_ref[pl.ds(where, 2 * row_count), :] = left.astype(jnp.bfloat16)
                for half in range(2):
                    lanes = slice(half * BLOCK, (half + 1) * BLOCK)
                    right_ref[(at + first) * 2 + half, :, :BLOCK] = rows[:, lanes]
                    right_ref[(at + first) * 2 + half, :, BLOCK:] = turned[:, lanes]
                return carry

            lax.fori_loop(0, pairs, body, 0, unroll=4)
            return pairs

        prepare(high, prepare(low, 0))

    for tile in range(tiles):
        at = step * tiles + tile
        left_at = pl.multiple_of(rows_ref[at] * row_count, row_count)
        product = jnp.dot(
            left_ref[pl.ds(left_at, row_count), :],
            right_ref[cols_ref[at]],
            preferred_element_type=jnp.float32,
        )
        product = product * scale
        out_ref[tile, 0, 0] = product[:, :BLOCK]
        out_ref[tile, 0, 1] = product[:, BLOCK:]


def stack_bin(freq, out_shape, tile_rows, tile_cols, whole, split, scale, so_far):
    low = [pair[0] for pair in split]
    high = [pair[1] for pair in split]
    pieces = whole + low + high
    channels = whole[0].shape[1]
    depth = sum(value.shape[0] for value in whole + low)
    tile_total, _, parts, row_count, _ = out_shape.shape
    tiles = max(size for size in range(1, 17) if tile_total % size == 0)
    blocks = channels // BLOCK
    in_specs = [
        pl.BlockSpec(value.shape, lambda step, *_: (0, 0), pipeline_mode=pl.Buffered(1))
        for value in pieces
    ]
    operands = [tile_rows, tile_cols] + pieces
    aliases = {}
    if so_far is not None:
        in_specs.append(pl.BlockSpec(memory_space=pl.ANY))
        aliases = {len(operands): 0}
        operands.append(so_far)
    block = (tiles, 1, parts, row_count, BLOCK)
    scratch = [
        pltpu.VMEM((blocks * row_count, depth), jnp.bfloat16),
        pltpu.VMEM((blocks, depth, 2 * BLOCK), jnp.bfloat16),
    ]
    product = tile_total * row_count * 2 * BLOCK
    return pl.pallas_call(
        functools.partial(stack_kernel, (len(whole), len(split), len(aliases)), row_count, scale),
        out_shape=out_shape,
        grid_spec=pltpu.PrefetchScalarGridSpec(
            num_scalar_prefetch=2,
            grid=(tile_total // tiles,),
            in_specs=in_specs,
            out_specs=pl.BlockSpec(block, lambda step, *_: (step, freq, 0, 0, 0)),
            scratch_shapes=scratch,
        ),
        input_output_aliases=aliases,
        cost_estimate=pl.CostEstimate(
            flops=2 * product * depth, bytes_accessed=4 * product, transcendentals=0
        ),
        compiler_params=pltpu.CompilerParams(vmem_limit_bytes=56 * 1024 * 1024),
        name="stack",
    )(*operands)


def on_device(spectra, tile_rows, tile_cols):
    window_total = (
        spectra.shape[2] * lax.axis_size("row") * lax.axis_size("col") * lax.axis_size("win")
    )
    scale = float(1.0 / window_total**0.5)
    slabs = whiten(spectra[0])
    row_count = BLOCK // lax.axis_size("win")
    out_shape = jax.ShapeDtypeStruct(
        (tile_rows.shape[0], len(slabs), 2, row_count, BLOCK), jnp.float32
    )
    gathered = [gather_windows(slab) for slab in slabs]
    out = None
    for freq, (whole, split) in enumerate(gathered):
        out = stack_bin(freq, out_shape, tile_rows, tile_cols, whole, split, scale, out)
    return out


def solution(mesh):
    in_specs = (P("win", None, ("row", "col"), None, None), P(("row", "col")), P(("row", "col")))
    out_specs = P(("row", "col"), None, None, "win", None)
    return jax.shard_map(
        on_device, mesh=mesh, in_specs=in_specs, out_specs=out_specs, check_vma=False
    )
```

```python
import functools
import math

import jax
import jax.numpy as jnp
from jax import lax
from jax.experimental import pallas as pl
from jax.experimental.pallas import tpu as pltpu
from jax.sharding import PartitionSpec as P

BLOCK = 128
MXU = 256


def whiten_kernel(spectra_ref, *out_refs):
    freqs = spectra_ref.shape[0]
    power = None
    for freq in range(freqs):
        slab = spectra_ref[freq]
        term = jnp.sum(slab * slab, axis=1, keepdims=True)
        power = term if power is None else power + term
    floor = jnp.maximum(jnp.sqrt(power / freqs), 1.0)
    for freq in range(freqs):
        out_refs[freq][...] = (spectra_ref[freq] / floor).astype(jnp.bfloat16)


def whiten(spectra):
    freqs, windows, parts, channels = spectra.shape
    shape = jax.ShapeDtypeStruct((windows, parts, channels), jnp.bfloat16)
    slabs = pl.pallas_call(whiten_kernel, out_shape=[shape] * freqs, name="whiten")(spectra)
    return [slab.reshape(windows * parts, channels) for slab in slabs]


def shift(value, axis, step, inner=1):
    size = lax.axis_size(axis)
    stops = size // inner
    perm = [(at, (at // inner + step) % stops * inner + at % inner) for at in range(size)]
    return lax.ppermute(value, axis, perm)


def gather_line(own):
    line = [own] + [shift(own, "col", step) for step in range(1, lax.axis_size("col"))]
    return jnp.concatenate(line, axis=0)


def row_cores():
    return 2 if lax.axis_size("row") % 2 == 0 else 1


def gather_cross(block):
    cores = row_cores()
    along_row = [
        shift(block, "row", step, cores) for step in range(1, lax.axis_size("row") // cores)
    ]
    along_win = [shift(block, "win", step) for step in range(1, lax.axis_size("win"))]
    return along_row, along_win


def gather_rest(block, along_row, along_win):
    cores = row_cores()
    half = block.shape[1] // 2
    whole = [block] + along_row + along_win
    split = []
    for row_step, from_row in enumerate(along_row, 1):
        for win_step, from_win in enumerate(along_win, 1):
            low = shift(from_win[:, :half], "row", row_step, cores)
            high = shift(from_row[:, half:], "win", win_step)
            split.append((low, high))
    if cores == 2:
        swap = functools.partial(
            lax.ppermute,
            axis_name="row",
            perm=[(at, at ^ 1) for at in range(lax.axis_size("row"))],
        )
        whole = whole + [swap(value) for value in whole]
        split = split + [(swap(low), swap(high)) for low, high in split]
    return whole, split


def gather_windows(slabs):
    gathered = []
    after = None
    for own in slabs:
        if after is not None:
            own, after = lax.optimization_barrier((own, after[0])), after[1]
            own = own[0]
        block = gather_line(own)
        sent = block
        if after is not None:
            sent = lax.optimization_barrier((block, after))[0]
        along_row, along_win = gather_cross(sent)
        gathered.append(gather_rest(block, along_row, along_win))
        after = (block, along_row + along_win)
    return gathered


def stack_kernel(counts, freq, scale, pack, rows_ref, cols_ref, *refs):
    whole_count, split_count, aliased = counts
    whole = refs[:whole_count]
    low = refs[whole_count : whole_count + split_count]
    high = refs[whole_count + split_count : whole_count + 2 * split_count]
    out_ref, left_ref, right_ref, ring_ref, sems = refs[whole_count + 2 * split_count + aliased :]
    copies, _, width = left_ref.shape
    depth = right_ref.shape[1]
    slots, tiles, _, row_count, _ = ring_ref.shape
    chunks = pack // copies

    offset = lax.axis_index("win") * row_count
    pick_at = lax.broadcasted_iota(jnp.int32, (2 * row_count, 2 * BLOCK), 0)
    pick_lane = lax.broadcasted_iota(jnp.int32, (2 * row_count, 2 * BLOCK), 1)
    want = pick_at % row_count + offset + pick_at // row_count * BLOCK
    pick = (pick_lane == want).astype(jnp.bfloat16)
    turn_at = lax.broadcasted_iota(jnp.int32, (depth, depth), 0)
    turn_lane = lax.broadcasted_iota(jnp.int32, (depth, depth), 1)
    turn = jnp.where(
        turn_at % 2 == 1,
        jnp.where(turn_lane == turn_at - 1, -1.0, 0.0),
        jnp.where(turn_lane == turn_at + 1, 1.0, 0.0),
    ).astype(jnp.bfloat16)
    place = lax.broadcasted_iota(jnp.int32, (2 * row_count, width), 1) // depth

    def prepare(halves, first, pairs):
        def body(at, carry):
            here = pl.multiple_of((at + first) * 2 * BLOCK, 2 * BLOCK)
            near = pl.multiple_of(at * 2 * BLOCK, 2 * BLOCK)
            pieces = [ref[:, pl.ds(here, 2 * BLOCK)] for ref in whole]
            pieces += [ref[:, pl.ds(near, 2 * BLOCK)] for ref in halves]
            rows = jnp.concatenate(pieces, axis=0)
            turned = jnp.dot(turn, rows, preferred_element_type=jnp.float32).astype(jnp.bfloat16)
            left = lax.dot_general(
                pick,
                jnp.concatenate([rows] * copies, axis=0),
                (((1,), (1,)), ((), ())),
                preferred_element_type=jnp.float32,
            )
            where = pl.multiple_of((at + first) * 2 * row_count, 2 * row_count)
            for copy in range(copies):
                only = left if copies == 1 else jnp.where(place == copy, left, 0.0)
                left_ref[copy, pl.ds(where, 2 * row_count), :] = only.astype(jnp.bfloat16)
            for half in range(2):
                lanes = slice(half * BLOCK, (half + 1) * BLOCK)
                right_ref[(at + first) * 2 + half, :, :BLOCK] = rows[:, lanes]
                right_ref[(at + first) * 2 + half, :, BLOCK:] = turned[:, lanes]
            return carry

        lax.fori_loop(0, pairs, body, 0, unroll=8 if pairs % 8 == 0 else 1)

    half_pairs = whole[0].shape[1] // (4 * BLOCK)
    prepare(low, 0, half_pairs)
    prepare(high, half_pairs, half_pairs)

    def send(step, slot):
        return pltpu.make_async_copy(
            ring_ref.at[slot], out_ref.at[pl.ds(step * tiles, tiles), freq], sems.at[slot]
        )

    steps = out_ref.shape[0] // tiles

    def stack(step, carry):
        slot = lax.rem(step, slots)

        @pl.when(step >= slots)
        def _():
            send(step - slots, slot).wait()

        for group in range(tiles // pack):
            lefts = []
            rights = []
            for member in range(pack):
                at = step * tiles + group * pack + member
                left_at = pl.multiple_of(rows_ref[at] * row_count, row_count)
                left = left_ref[member % copies, pl.ds(left_at, row_count), :]
                if chunks > 1:
                    chunk = member // copies
                    empty = jnp.zeros_like(left)
                    left = jnp.concatenate(
                        [left if spot == chunk else empty for spot in range(chunks)], axis=1
                    )
                lefts.append(left)
                rights.append(right_ref[cols_ref[at]])
            product = jnp.dot(
                jnp.concatenate(lefts, axis=0),
                jnp.concatenate(rights, axis=0),
                preferred_element_type=jnp.float32,
            )
            product = product * scale
            for member in range(pack):
                mine = product[member * row_count : (member + 1) * row_count]
                ring_ref[slot, group * pack + member, 0] = mine[:, :BLOCK]
                ring_ref[slot, group * pack + member, 1] = mine[:, BLOCK:]
        send(step, slot).start()
        return carry

    lax.fori_loop(0, steps, stack, 0)
    for step in range(max(0, steps - slots), steps):
        send(step, step % slots).wait()


def stack_bin(freq, out_shape, tile_rows, tile_cols, whole, split, scale, so_far):
    low = [pair[0] for pair in split]
    high = [pair[1] for pair in split]
    pieces = whole + low + high
    channels = whole[0].shape[1]
    depth = sum(value.shape[0] for value in whole + low)
    tile_total, _, parts, row_count, _ = out_shape.shape
    pack = math.gcd(tile_total, max(1, MXU // depth))
    copies = min(pack, max(1, BLOCK // depth))
    tiles = max(size for size in range(pack, pack + 13) if tile_total % size + size % pack == 0)
    blocks = channels // BLOCK
    vmem = pl.BlockSpec(memory_space=pltpu.VMEM)
    smem = pl.BlockSpec(memory_space=pltpu.SMEM)
    in_specs = [smem, smem] + [vmem] * len(pieces)
    operands = [tile_rows, tile_cols] + pieces
    aliases = {}
    if so_far is not None:
        in_specs.append(pl.BlockSpec(memory_space=pl.ANY))
        aliases = {len(operands): 0}
        operands.append(so_far)
    slots = 4
    scratch = [
        ((copies, blocks * row_count, copies * depth), jnp.bfloat16),
        ((blocks, depth, 2 * BLOCK), jnp.bfloat16),
        ((slots, tiles, parts, row_count, BLOCK), jnp.float32),
    ]
    used = [(value.shape, value.dtype) for value in pieces] + scratch
    vmem_bytes = sum(math.prod(shape) * jnp.dtype(kind).itemsize for shape, kind in used)
    product = tile_total * row_count * 2 * BLOCK
    return pl.pallas_call(
        functools.partial(stack_kernel, (len(whole), len(split), len(aliases)), freq, scale, pack),
        out_shape=out_shape,
        in_specs=in_specs,
        out_specs=pl.BlockSpec(memory_space=pl.ANY),
        scratch_shapes=[pltpu.VMEM(*spec) for spec in scratch]
        + [pltpu.SemaphoreType.DMA((slots,))],
        input_output_aliases=aliases,
        cost_estimate=pl.CostEstimate(
            flops=2 * product * depth, bytes_accessed=4 * product, transcendentals=0
        ),
        compiler_params=pltpu.CompilerParams(vmem_limit_bytes=vmem_bytes + 8 * 1024 * 1024),
        name="stack",
    )(*operands)


def on_device(spectra, tile_rows, tile_cols):
    window_total = (
        spectra.shape[2] * lax.axis_size("row") * lax.axis_size("col") * lax.axis_size("win")
    )
    scale = float(1.0 / window_total**0.5)
    slabs = whiten(spectra[0])
    row_count = BLOCK // lax.axis_size("win")
    out_shape = jax.ShapeDtypeStruct(
        (tile_rows.shape[0], len(slabs), 2, row_count, BLOCK), jnp.float32
    )
    out = None
    for freq, (whole, split) in enumerate(gather_windows(slabs)):
        out = stack_bin(freq, out_shape, tile_rows, tile_cols, whole, split, scale, out)
    return out


def solution(mesh):
    in_specs = (P("win", None, ("row", "col"), None, None), P(("row", "col")), P(("row", "col")))
    out_specs = P(("row", "col"), None, None, "win", None)
    return jax.shard_map(
        on_device, mesh=mesh, in_specs=in_specs, out_specs=out_specs, check_vma=False
    )
```

```python
import functools
import math

import jax
import jax.numpy as jnp
from jax import lax
from jax.experimental import pallas as pl
from jax.experimental.pallas import tpu as pltpu
from jax.sharding import PartitionSpec as P

BLOCK = 128
MXU = 256


def whiten_kernel(spectra_ref, *out_refs):
    freqs = spectra_ref.shape[0]
    power = None
    for freq in range(freqs):
        slab = spectra_ref[freq]
        term = jnp.sum(slab * slab, axis=1, keepdims=True)
        power = term if power is None else power + term
    floor = jnp.maximum(jnp.sqrt(power / freqs), 1.0)
    for freq in range(freqs):
        out_refs[freq][...] = (spectra_ref[freq] / floor).astype(jnp.bfloat16)


def whiten(spectra):
    freqs, windows, parts, channels = spectra.shape
    shape = jax.ShapeDtypeStruct((windows, parts, channels), jnp.bfloat16)
    slabs = pl.pallas_call(whiten_kernel, out_shape=[shape] * freqs, name="whiten")(spectra)
    return [slab.reshape(windows * parts, channels) for slab in slabs]


def shift(value, axis, step, inner=1):
    size = lax.axis_size(axis)
    stops = size // inner
    perm = [(at, (at // inner + step) % stops * inner + at % inner) for at in range(size)]
    return lax.ppermute(value, axis, perm)


def shift_plane(value, row_step, win_step, inner):
    row_size, win_size = lax.axis_size("row"), lax.axis_size("win")
    stops = row_size // inner
    perm = []
    for row in range(row_size):
        for win in range(win_size):
            to_row = (row // inner + row_step) % stops * inner + row % inner
            perm.append((row * win_size + win, to_row * win_size + (win + win_step) % win_size))
    return lax.ppermute(value, ("row", "win"), perm)


def gather_line(own):
    line = [own] + [shift(own, "col", step) for step in range(1, lax.axis_size("col"))]
    return jnp.concatenate(line, axis=0)


def row_cores():
    return 2 if lax.axis_size("row") % 2 == 0 else 1


def gather_cross(block):
    cores = row_cores()
    stops = lax.axis_size("row") // cores
    blocks = []
    for win_step in range(lax.axis_size("win")):
        for row_step in range(stops):
            if row_step + win_step > 0:
                blocks.append(shift_plane(block, row_step, win_step, cores))
    return blocks


def swap_cores(value):
    return lax.ppermute(value, "row", [(at, at ^ 1) for at in range(lax.axis_size("row"))])


def after(value, *earlier):
    return lax.optimization_barrier((value, *earlier))[0]


def stack_kernel(counts, freq, scale, pack, lists_hbm, *refs):
    piece_count, aliased = counts
    pieces = refs[:piece_count]
    out_ref, left_ref, right_ref, ring_ref, lists_ref, sems, list_sem = refs[
        piece_count + aliased :
    ]
    total = out_ref.shape[0]
    copies, _, width = left_ref.shape
    depth = right_ref.shape[1]
    slots, tiles, _, row_count, _ = ring_ref.shape
    chunks = pack // copies

    lists = pltpu.make_async_copy(lists_hbm, lists_ref, list_sem)
    lists.start()

    offset = lax.axis_index("win") * row_count
    pick_at = lax.broadcasted_iota(jnp.int32, (2 * row_count, 2 * BLOCK), 0)
    pick_lane = lax.broadcasted_iota(jnp.int32, (2 * row_count, 2 * BLOCK), 1)
    want = pick_at % row_count + offset + pick_at // row_count * BLOCK
    pick = (pick_lane == want).astype(jnp.bfloat16)
    turn_at = lax.broadcasted_iota(jnp.int32, (depth, depth), 0)
    turn_lane = lax.broadcasted_iota(jnp.int32, (depth, depth), 1)
    turn = jnp.where(
        turn_at % 2 == 1,
        jnp.where(turn_lane == turn_at - 1, -1.0, 0.0),
        jnp.where(turn_lane == turn_at + 1, 1.0, 0.0),
    ).astype(jnp.bfloat16)
    place = lax.broadcasted_iota(jnp.int32, (2 * row_count, width), 1) // depth

    def prepare(at, carry):
        here = pl.multiple_of(at * 2 * BLOCK, 2 * BLOCK)
        rows = jnp.concatenate([ref[:, pl.ds(here, 2 * BLOCK)] for ref in pieces], axis=0)
        turned = jnp.dot(turn, rows, preferred_element_type=jnp.float32).astype(jnp.bfloat16)
        left = lax.dot_general(
            pick,
            jnp.concatenate([rows] * copies, axis=0),
            (((1,), (1,)), ((), ())),
            preferred_element_type=jnp.float32,
        )
        where = pl.multiple_of(at * 2 * row_count, 2 * row_count)
        for copy in range(copies):
            only = left if copies == 1 else jnp.where(place == copy, left, 0.0)
            left_ref[copy, pl.ds(where, 2 * row_count), :] = only.astype(jnp.bfloat16)
        for half in range(2):
            lanes = slice(half * BLOCK, (half + 1) * BLOCK)
            right_ref[at * 2 + half, :, :BLOCK] = rows[:, lanes]
            right_ref[at * 2 + half, :, BLOCK:] = turned[:, lanes]
        return carry

    pairs = pieces[0].shape[1] // (2 * BLOCK)
    lax.fori_loop(0, pairs, prepare, 0, unroll=8 if pairs % 8 == 0 else 1)
    lists.wait()

    def send(step, slot, count=tiles):
        return pltpu.make_async_copy(
            ring_ref.at[slot, pl.ds(0, count)],
            out_ref.at[pl.ds(step * tiles, count), freq],
            sems.at[slot],
        )

    def compute(step, slot, count):
        for group in range(count // pack):
            lefts = []
            rights = []
            for member in range(pack):
                at = step * tiles + group * pack + member
                left_at = pl.multiple_of(lists_ref[at] * row_count, row_count)
                left = left_ref[member % copies, pl.ds(left_at, row_count), :]
                if chunks > 1:
                    chunk = member // copies
                    empty = jnp.zeros_like(left)
                    left = jnp.concatenate(
                        [left if spot == chunk else empty for spot in range(chunks)], axis=1
                    )
                lefts.append(left)
                rights.append(right_ref[lists_ref[total + at]])
            product = jnp.dot(
                jnp.concatenate(lefts, axis=0),
                jnp.concatenate(rights, axis=0),
                preferred_element_type=jnp.float32,
            )
            product = product * scale
            for member in range(pack):
                mine = product[member * row_count : (member + 1) * row_count]
                ring_ref[slot, group * pack + member, 0] = mine[:, :BLOCK]
                ring_ref[slot, group * pack + member, 1] = mine[:, BLOCK:]

    steps = total // tiles
    rest = total % tiles

    def stack(step, carry):
        slot = lax.rem(step, slots)

        @pl.when(step >= slots)
        def _():
            send(step - slots, slot).wait()

        compute(step, slot, tiles)
        send(step, slot).start()
        return carry

    lax.fori_loop(0, steps, stack, 0)
    sent = [(step, tiles) for step in range(max(0, steps - slots), steps)]
    if rest:
        if steps >= slots:
            send(sent[0][0], sent[0][0] % slots).wait()
            sent = sent[1:]
        compute(steps, steps % slots, rest)
        send(steps, steps % slots, rest).start()
        sent.append((steps, rest))
    for step, count in sent:
        send(step, step % slots, count).wait()


def stack_bin(freq, out_shape, lists, pieces, scale, so_far):
    channels = pieces[0].shape[1]
    depth = sum(value.shape[0] for value in pieces)
    tile_total, _, parts, row_count, _ = out_shape.shape
    pack = math.gcd(tile_total, max(1, MXU // depth))
    copies = min(pack, max(1, BLOCK // depth))
    tiles = max(pack, 24 // pack * pack)
    tiles = min(tiles, tile_total)
    blocks = channels // BLOCK
    vmem = pl.BlockSpec(memory_space=pltpu.VMEM)
    in_specs = [pl.BlockSpec(memory_space=pl.ANY)] + [vmem] * len(pieces)
    operands = [lists] + pieces
    aliases = {}
    if so_far is not None:
        in_specs.append(pl.BlockSpec(memory_space=pl.ANY))
        aliases = {len(operands): 0}
        operands.append(so_far)
    slots = 4
    scratch = [
        ((copies, blocks * row_count, copies * depth), jnp.bfloat16),
        ((blocks, depth, 2 * BLOCK), jnp.bfloat16),
        ((slots, tiles, parts, row_count, BLOCK), jnp.float32),
    ]
    used = [(value.shape, value.dtype) for value in pieces] + scratch
    vmem_bytes = sum(math.prod(shape) * jnp.dtype(kind).itemsize for shape, kind in used)
    product = tile_total * row_count * 2 * BLOCK
    return pl.pallas_call(
        functools.partial(stack_kernel, (len(pieces), len(aliases)), freq, scale, pack),
        out_shape=out_shape,
        in_specs=in_specs,
        out_specs=pl.BlockSpec(memory_space=pl.ANY),
        scratch_shapes=[pltpu.VMEM(*spec) for spec in scratch]
        + [pltpu.SMEM(lists.shape, jnp.int32)]
        + [pltpu.SemaphoreType.DMA((slots,)), pltpu.SemaphoreType.DMA],
        input_output_aliases=aliases,
        cost_estimate=pl.CostEstimate(
            flops=2 * product * depth, bytes_accessed=4 * product, transcendentals=0
        ),
        compiler_params=pltpu.CompilerParams(vmem_limit_bytes=vmem_bytes + 8 * 1024 * 1024),
        name="stack",
    )(*operands)


def on_device(spectra, tile_rows, tile_cols):
    window_total = (
        spectra.shape[2] * lax.axis_size("row") * lax.axis_size("col") * lax.axis_size("win")
    )
    scale = float(1.0 / window_total**0.5)
    slabs = whiten(spectra[0])
    row_count = BLOCK // lax.axis_size("win")
    out_shape = jax.ShapeDtypeStruct(
        (tile_rows.shape[0], len(slabs), 2, row_count, BLOCK), jnp.float32
    )
    lists = jnp.concatenate([tile_rows, tile_cols])
    out = None
    gate = None
    for freq, own in enumerate(slabs):
        if gate is not None:
            own = after(own, gate, lists)
        block = gather_line(own)
        swapped = [swap_cores(block)] if row_cores() == 2 else []
        gate = (swapped or [block])[0]
        sent = block if out is None else after(block, *arrived)
        arrived = gather_cross(sent)
        pieces = [block] + arrived
        if swapped:
            ready = arrived if out is None else after(tuple(arrived), out)
            swapped += [swap_cores(value) for value in ready]
        out = stack_bin(freq, out_shape, lists, pieces + swapped, scale, out)
    return out


def solution(mesh):
    in_specs = (P("win", None, ("row", "col"), None, None), P(("row", "col")), P(("row", "col")))
    out_specs = P(("row", "col"), None, None, "win", None)
    return jax.shard_map(
        on_device, mesh=mesh, in_specs=in_specs, out_specs=out_specs, check_vma=False
    )
```

```python
import functools
import math

import jax
import jax.numpy as jnp
from jax import lax
from jax.experimental import pallas as pl
from jax.experimental.pallas import tpu as pltpu
from jax.sharding import PartitionSpec as P

BLOCK = 128
MXU = 256


def whiten_kernel(spectra_ref, *out_refs):
    freqs = spectra_ref.shape[0]
    power = None
    for freq in range(freqs):
        slab = spectra_ref[freq]
        term = jnp.sum(slab * slab, axis=1, keepdims=True)
        power = term if power is None else power + term
    factor = jnp.minimum(lax.rsqrt(power / freqs), 1.0)
    for freq in range(freqs):
        out_refs[freq][...] = (spectra_ref[freq] * factor).astype(jnp.bfloat16)


def whiten(spectra):
    freqs, windows, parts, channels = spectra.shape
    shape = jax.ShapeDtypeStruct((windows, parts, channels), jnp.bfloat16)
    slabs = pl.pallas_call(whiten_kernel, out_shape=[shape] * freqs, name="whiten")(spectra)
    return [slab.reshape(windows * parts, channels) for slab in slabs]


def shift(value, axis, step, inner=1):
    size = lax.axis_size(axis)
    stops = size // inner
    perm = [(at, (at // inner + step) % stops * inner + at % inner) for at in range(size)]
    return lax.ppermute(value, axis, perm)


def shift_plane(value, row_step, win_step, inner):
    row_size, win_size = lax.axis_size("row"), lax.axis_size("win")
    stops = row_size // inner
    perm = []
    for row in range(row_size):
        for win in range(win_size):
            to_row = (row // inner + row_step) % stops * inner + row % inner
            perm.append((row * win_size + win, to_row * win_size + (win + win_step) % win_size))
    return lax.ppermute(value, ("row", "win"), perm)


def gather_line(own):
    line = [own] + [shift(own, "col", step) for step in range(1, lax.axis_size("col"))]
    return jnp.concatenate(line, axis=0)


def row_cores():
    return 2 if lax.axis_size("row") % 2 == 0 else 1


def gather_direct(block, earlier):
    cores = row_cores()
    sent = after(block, *earlier)
    blocks = []
    for win_step in range(lax.axis_size("win")):
        for row_step in range(lax.axis_size("row") // cores):
            if row_step + win_step > 0:
                blocks.append(shift_plane(sent, row_step, win_step, cores))
    return blocks


def gather_relayed(block):
    cores = row_cores()
    half = block.shape[1] // 2
    along_row = [
        shift(block, "row", step, cores) for step in range(1, lax.axis_size("row") // cores)
    ]
    along_win = [shift(block, "win", step) for step in range(1, lax.axis_size("win"))]
    lows = []
    highs = []
    for row_step, from_row in enumerate(along_row, 1):
        for win_step, from_win in enumerate(along_win, 1):
            lows.append(shift(from_win[:, :half], "row", row_step, cores))
            highs.append(shift(from_row[:, half:], "win", win_step))
    return along_row + along_win, lows, highs


def swap_cores(value):
    return lax.ppermute(value, "row", [(at, at ^ 1) for at in range(lax.axis_size("row"))])


def after(value, *earlier):
    return lax.optimization_barrier((value, *earlier))[0]


def stack_kernel(counts, freq, scale, pack, lists_hbm, *refs):
    whole_count, half_count, aliased = counts
    whole = refs[:whole_count]
    lows = refs[whole_count : whole_count + half_count]
    piece_count = whole_count + 2 * half_count
    highs = refs[whole_count + half_count : piece_count]
    out_ref, left_ref, right_ref, ring_ref, lists_ref, sems, list_sem = refs[
        piece_count + aliased :
    ]
    total = out_ref.shape[0]
    copies, _, width = left_ref.shape
    depth = right_ref.shape[1]
    slots, tiles, _, row_count, _ = ring_ref.shape
    chunks = pack // copies

    lists = pltpu.make_async_copy(lists_hbm, lists_ref, list_sem)
    lists.start()

    offset = lax.axis_index("win") * row_count
    pick_at = lax.broadcasted_iota(jnp.int32, (2 * row_count, 2 * BLOCK), 0)
    pick_lane = lax.broadcasted_iota(jnp.int32, (2 * row_count, 2 * BLOCK), 1)
    want = pick_at % row_count + offset + pick_at // row_count * BLOCK
    pick = (pick_lane == want).astype(jnp.bfloat16)
    turn_at = lax.broadcasted_iota(jnp.int32, (depth, depth), 0)
    turn_lane = lax.broadcasted_iota(jnp.int32, (depth, depth), 1)
    turn = jnp.where(
        turn_at % 2 == 1,
        jnp.where(turn_lane == turn_at - 1, -1.0, 0.0),
        jnp.where(turn_lane == turn_at + 1, 1.0, 0.0),
    ).astype(jnp.bfloat16)
    place = lax.broadcasted_iota(jnp.int32, (2 * row_count, width), 1) // depth

    def prepare(first, halves, at, carry):
        near = pl.ds(pl.multiple_of(at * 2 * BLOCK, 2 * BLOCK), 2 * BLOCK)
        at = at + first
        here = pl.ds(pl.multiple_of(at * 2 * BLOCK, 2 * BLOCK), 2 * BLOCK)
        pieces = [ref[:, here] for ref in whole] + [ref[:, near] for ref in halves]
        rows = jnp.concatenate(pieces, axis=0)
        turned = jnp.dot(turn, rows, preferred_element_type=jnp.float32).astype(jnp.bfloat16)
        left = lax.dot_general(
            pick,
            jnp.concatenate([rows] * copies, axis=0),
            (((1,), (1,)), ((), ())),
            preferred_element_type=jnp.float32,
        )
        where = pl.multiple_of(at * 2 * row_count, 2 * row_count)
        for copy in range(copies):
            only = left if copies == 1 else jnp.where(place == copy, left, 0.0)
            left_ref[copy, pl.ds(where, 2 * row_count), :] = only.astype(jnp.bfloat16)
        for half in range(2):
            lanes = slice(half * BLOCK, (half + 1) * BLOCK)
            right_ref[at * 2 + half, :, :BLOCK] = rows[:, lanes]
            right_ref[at * 2 + half, :, BLOCK:] = turned[:, lanes]
        return carry

    pairs = whole[0].shape[1] // (2 * BLOCK)
    runs = [(0, lows), (pairs // 2, highs)] if half_count else [(0, [])]
    for first, halves in runs:
        count = pairs // len(runs)
        body = functools.partial(prepare, first, halves)
        lax.fori_loop(0, count, body, 0, unroll=8 if count % 8 == 0 else 1)
    lists.wait()

    def send(step, slot, count=tiles):
        return pltpu.make_async_copy(
            ring_ref.at[slot, pl.ds(0, count)],
            out_ref.at[pl.ds(step * tiles, count), freq],
            sems.at[slot],
        )

    def compute(step, slot, count):
        for group in range(count // pack):
            lefts = []
            rights = []
            for member in range(pack):
                at = step * tiles + group * pack + member
                left_at = pl.multiple_of(lists_ref[at] * row_count, row_count)
                left = left_ref[member % copies, pl.ds(left_at, row_count), :]
                if chunks > 1:
                    chunk = member // copies
                    empty = jnp.zeros_like(left)
                    left = jnp.concatenate(
                        [left if spot == chunk else empty for spot in range(chunks)], axis=1
                    )
                lefts.append(left)
                rights.append(right_ref[lists_ref[total + at]])
            product = jnp.dot(
                jnp.concatenate(lefts, axis=0),
                jnp.concatenate(rights, axis=0),
                preferred_element_type=jnp.float32,
            )
            product = product * scale
            for member in range(pack):
                mine = product[member * row_count : (member + 1) * row_count]
                ring_ref[slot, group * pack + member, 0] = mine[:, :BLOCK]
                ring_ref[slot, group * pack + member, 1] = mine[:, BLOCK:]

    steps = total // tiles
    rest = total % tiles

    def stack(step, carry):
        slot = lax.rem(step, slots)

        @pl.when(step >= slots)
        def _():
            send(step - slots, slot).wait()

        compute(step, slot, tiles)
        send(step, slot).start()
        return carry

    lax.fori_loop(0, steps, stack, 0)
    sent = [(step, tiles) for step in range(max(0, steps - slots), steps)]
    if rest:
        if steps >= slots:
            send(sent[0][0], sent[0][0] % slots).wait()
            sent = sent[1:]
        compute(steps, steps % slots, rest)
        send(steps, steps % slots, rest).start()
        sent.append((steps, rest))
    for step, count in sent:
        send(step, step % slots, count).wait()


def stack_bin(freq, out_shape, lists, whole, lows, highs, scale, so_far):
    pieces = whole + lows + highs
    channels = whole[0].shape[1]
    depth = sum(value.shape[0] for value in whole + lows)
    tile_total, _, parts, row_count, _ = out_shape.shape
    pack = math.gcd(tile_total, max(1, MXU // depth))
    copies = min(pack, max(1, BLOCK // depth))
    tiles = max(pack, 48 // pack * pack)
    tiles = min(tiles, tile_total)
    blocks = channels // BLOCK
    vmem = pl.BlockSpec(memory_space=pltpu.VMEM)
    in_specs = [pl.BlockSpec(memory_space=pl.ANY)] + [vmem] * len(pieces)
    operands = [lists] + pieces
    aliases = {}
    if so_far is not None:
        in_specs.append(pl.BlockSpec(memory_space=pl.ANY))
        aliases = {len(operands): 0}
        operands.append(so_far)
    slots = 3
    scratch = [
        ((copies, blocks * row_count, copies * depth), jnp.bfloat16),
        ((blocks, depth, 2 * BLOCK), jnp.bfloat16),
        ((slots, tiles, parts, row_count, BLOCK), jnp.float32),
    ]
    used = [(value.shape, value.dtype) for value in pieces] + scratch
    vmem_bytes = sum(math.prod(shape) * jnp.dtype(kind).itemsize for shape, kind in used)
    product = tile_total * row_count * 2 * BLOCK
    return pl.pallas_call(
        functools.partial(stack_kernel, (len(whole), len(lows), len(aliases)), freq, scale, pack),
        out_shape=out_shape,
        in_specs=in_specs,
        out_specs=pl.BlockSpec(memory_space=pl.ANY),
        scratch_shapes=[pltpu.VMEM(*spec) for spec in scratch]
        + [pltpu.SMEM(lists.shape, jnp.int32)]
        + [pltpu.SemaphoreType.DMA((slots,)), pltpu.SemaphoreType.DMA],
        input_output_aliases=aliases,
        cost_estimate=pl.CostEstimate(
            flops=2 * product * depth, bytes_accessed=4 * product, transcendentals=0
        ),
        compiler_params=pltpu.CompilerParams(vmem_limit_bytes=vmem_bytes + 8 * 1024 * 1024),
        name="stack",
    )(*operands)


def on_device(spectra, tile_rows, tile_cols):
    window_total = (
        spectra.shape[2] * lax.axis_size("row") * lax.axis_size("col") * lax.axis_size("win")
    )
    scale = float(1.0 / window_total**0.5)
    slabs = whiten(spectra[0])
    row_count = BLOCK // lax.axis_size("win")
    out_shape = jax.ShapeDtypeStruct(
        (tile_rows.shape[0], len(slabs), 2, row_count, BLOCK), jnp.float32
    )
    lists = jnp.concatenate([tile_rows, tile_cols])
    swap = swap_cores if row_cores() == 2 else None
    out = None
    for freq, own in enumerate(slabs):
        if freq > 0:
            own = after(own, gate, lists)
        block = gather_line(own)
        whole = [block]
        if swap:
            whole.append(swap(block))
        gate = whole[-1]
        if freq == 0:
            arrived, lows, highs = gather_relayed(block)
            last = lows + highs if lows else arrived
        else:
            arrived, lows, highs = gather_direct(block, last), [], []
            last = arrived
        if swap:
            ready = arrived if out is None else after(tuple(arrived), out)
            whole += [swap(value) for value in ready]
            lows = lows + [swap(value) for value in lows]
            highs = highs + [swap(value) for value in highs]
        out = stack_bin(freq, out_shape, lists, whole + arrived, lows, highs, scale, out)
    return out


def solution(mesh):
    in_specs = (P("win", None, ("row", "col"), None, None), P(("row", "col")), P(("row", "col")))
    out_specs = P(("row", "col"), None, None, "win", None)
    return jax.shard_map(
        on_device, mesh=mesh, in_specs=in_specs, out_specs=out_specs, check_vma=False
    )
```

```python
import functools
import math

import jax
import jax.numpy as jnp
from jax import lax
from jax.experimental import pallas as pl
from jax.experimental.pallas import tpu as pltpu
from jax.sharding import PartitionSpec as P

BLOCK = 128
MXU = 256


def whiten_kernel(spectra_ref, *out_refs):
    freqs = spectra_ref.shape[0]
    power = None
    for freq in range(freqs):
        slab = spectra_ref[freq]
        term = jnp.sum(slab * slab, axis=1, keepdims=True)
        power = term if power is None else power + term
    factor = jnp.minimum(lax.rsqrt(power / freqs), 1.0)
    for freq in range(freqs):
        out_refs[freq][...] = (spectra_ref[freq] * factor).astype(jnp.bfloat16)


def whiten(spectra):
    freqs, windows, parts, channels = spectra.shape
    shape = jax.ShapeDtypeStruct((windows, parts, channels), jnp.bfloat16)
    slabs = pl.pallas_call(whiten_kernel, out_shape=[shape] * freqs, name="whiten")(spectra)
    return [slab.reshape(windows * parts, channels) for slab in slabs]


def shift(value, axis, step):
    size = lax.axis_size(axis)
    return lax.ppermute(value, axis, [(at, (at + step) % size) for at in range(size)])


def gather_line(own):
    line = [own] + [shift(own, "col", step) for step in range(1, lax.axis_size("col"))]
    return jnp.concatenate(line, axis=0)


def gather_chips(own):
    return lax.all_gather(own, ("chip", "col", "win"), axis=0, tiled=True)


def by_column(tile_rows, tile_cols):
    total = tile_rows.shape[0]
    place = jnp.arange(total, dtype=jnp.int32)
    key = tile_cols * total + place
    rank = jnp.sum((key[None, :] < key[:, None]).astype(jnp.int32), axis=1)
    hit = rank[None, :] == place[:, None]
    return jnp.concatenate(
        [
            jnp.sum(jnp.where(hit, values[None, :], 0), axis=1)
            for values in (tile_rows, tile_cols, place)
        ]
    )


def gather_relayed(block):
    half = block.shape[1] // 2
    along_chip = [shift(block, "chip", step) for step in range(1, lax.axis_size("chip"))]
    along_win = [shift(block, "win", step) for step in range(1, lax.axis_size("win"))]
    lows = []
    highs = []
    for chip_step, from_chip in enumerate(along_chip, 1):
        for win_step, from_win in enumerate(along_win, 1):
            lows.append(shift(from_win[:, :half], "chip", chip_step))
            highs.append(shift(from_chip[:, half:], "win", win_step))
    return along_chip + along_win, lows, highs


def swap_cores(values):
    return [shift(value, "core", 1) for value in values] if lax.axis_size("core") == 2 else []


def stack_kernel(counts, freq, scale, pack, lists_hbm, *refs):
    whole_count, half_count, aliased = counts
    whole = refs[:whole_count]
    lows = refs[whole_count : whole_count + half_count]
    piece_count = whole_count + 2 * half_count
    highs = refs[whole_count + half_count : piece_count]
    out_ref, left_ref, right_ref, ring_ref, lists_ref, sems, list_sem = refs[
        piece_count + aliased :
    ]
    total = out_ref.shape[0]
    copies, _, width = left_ref.shape
    depth = right_ref.shape[1]
    slots, tiles, _, row_count, _ = ring_ref.shape
    chunks = pack // copies

    lists = pltpu.make_async_copy(lists_hbm, lists_ref, list_sem)
    lists.start()

    offset = lax.axis_index("win") * row_count
    pick_at = lax.broadcasted_iota(jnp.int32, (2 * row_count, 2 * BLOCK), 0)
    pick_lane = lax.broadcasted_iota(jnp.int32, (2 * row_count, 2 * BLOCK), 1)
    want = pick_at % row_count + offset + pick_at // row_count * BLOCK
    pick = (pick_lane == want).astype(jnp.bfloat16)
    turn_at = lax.broadcasted_iota(jnp.int32, (depth, depth), 0)
    turn_lane = lax.broadcasted_iota(jnp.int32, (depth, depth), 1)
    turn = jnp.where(
        turn_at % 2 == 1,
        jnp.where(turn_lane == turn_at - 1, -1.0, 0.0),
        jnp.where(turn_lane == turn_at + 1, 1.0, 0.0),
    ).astype(jnp.bfloat16)
    place = lax.broadcasted_iota(jnp.int32, (2 * row_count, width), 1) // depth

    def prepare(halves, first, at):
        near = pl.ds(pl.multiple_of((at - first) * 2 * BLOCK, 2 * BLOCK), 2 * BLOCK)
        here = pl.ds(pl.multiple_of(at * 2 * BLOCK, 2 * BLOCK), 2 * BLOCK)
        pieces = [ref[:, here] for ref in whole] + [ref[:, near] for ref in halves]
        rows = jnp.concatenate(pieces, axis=0)
        turned = jnp.dot(turn, rows, preferred_element_type=jnp.float32).astype(jnp.bfloat16)
        left = lax.dot_general(
            pick,
            jnp.concatenate([rows] * copies, axis=0),
            (((1,), (1,)), ((), ())),
            preferred_element_type=jnp.float32,
        )
        where = pl.multiple_of(at * 2 * row_count, 2 * row_count)
        for copy in range(copies):
            only = left if copies == 1 else jnp.where(place == copy, left, 0.0)
            left_ref[copy, pl.ds(where, 2 * row_count), :] = only.astype(jnp.bfloat16)
        for half in range(2):
            lanes = slice(half * BLOCK, (half + 1) * BLOCK)
            right_ref[at * 2 + half, :, :BLOCK] = rows[:, lanes]
            right_ref[at * 2 + half, :, BLOCK:] = turned[:, lanes]

    pairs = whole[0].shape[1] // (2 * BLOCK)
    span = math.gcd(pairs // 2, 8)
    parts = pairs // span

    def prepare_to(done, need):
        def part(halves, first, at, carry):
            for pair in range(span):
                prepare(halves, first, at * span + pair)
            return carry

        if not half_count:
            lax.fori_loop(done, need, functools.partial(part, [], 0), 0)
            return
        middle = parts // 2
        lax.fori_loop(done, jnp.minimum(need, middle), functools.partial(part, lows, 0), 0)
        first = functools.partial(part, highs, middle * span)
        lax.fori_loop(jnp.maximum(done, middle), need, first, 0)

    prepare_to(0, 1)
    lists.wait()

    def send(step, slot, count):
        for tile in range(count):
            to = lists_ref[2 * total + step * tiles + tile]
            pltpu.make_async_copy(
                ring_ref.at[slot, tile], out_ref.at[to, freq], sems.at[slot]
            ).start()

    def sent(slot, count):
        pltpu.make_async_copy(
            ring_ref.at[slot, pl.ds(0, count)], out_ref.at[pl.ds(0, count), freq], sems.at[slot]
        ).wait()

    def compute(step, slot, count):
        for group in range(count // pack):
            lefts = []
            rights = []
            for member in range(pack):
                at = step * tiles + group * pack + member
                left_at = pl.multiple_of(lists_ref[at] * row_count, row_count)
                left = left_ref[member % copies, pl.ds(left_at, row_count), :]
                if chunks > 1:
                    chunk = member // copies
                    empty = jnp.zeros_like(left)
                    left = jnp.concatenate(
                        [left if spot == chunk else empty for spot in range(chunks)], axis=1
                    )
                lefts.append(left)
                rights.append(right_ref[lists_ref[total + at]])
            product = jnp.dot(
                jnp.concatenate(lefts, axis=0),
                jnp.concatenate(rights, axis=0),
                preferred_element_type=jnp.float32,
            )
            product = product * scale
            for member in range(pack):
                mine = product[member * row_count : (member + 1) * row_count]
                ring_ref[slot, group * pack + member, 0] = mine[:, :BLOCK]
                ring_ref[slot, group * pack + member, 1] = mine[:, BLOCK:]

    steps = total // tiles
    rest = total % tiles

    def needed(last):
        return lists_ref[total + last] // (2 * span) + 1

    def stack(step, done):
        slot = lax.rem(step, slots)
        need = jnp.maximum(needed(step * tiles + tiles - 1), done)
        prepare_to(done, need)

        @pl.when(step >= slots)
        def _():
            sent(slot, tiles)

        compute(step, slot, tiles)
        send(step, slot, tiles)
        return need

    done = lax.fori_loop(0, steps, stack, jnp.int32(1))
    flying = [(step % slots, tiles) for step in range(max(0, steps - slots), steps)]
    if rest:
        prepare_to(done, needed(total - 1))
        slot = steps % slots
        if steps >= slots:
            sent(slot, tiles)
            flying = flying[1:]
        compute(steps, slot, rest)
        send(steps, slot, rest)
        flying.append((slot, rest))
    for slot, count in flying:
        sent(slot, count)


def stack_bin(freq, out_shape, lists, whole, lows, highs, scale, so_far):
    pieces = whole + lows + highs
    channels = whole[0].shape[1]
    depth = sum(value.shape[0] for value in whole + lows)
    tile_total, _, parts, row_count, _ = out_shape.shape
    pack = math.gcd(tile_total, max(1, MXU // depth))
    copies = min(pack, max(1, BLOCK // depth))
    tiles = max(pack, 24 // pack * pack)
    tiles = min(tiles, tile_total)
    blocks = channels // BLOCK
    vmem = pl.BlockSpec(memory_space=pltpu.VMEM)
    in_specs = [pl.BlockSpec(memory_space=pl.ANY)] + [vmem] * len(pieces)
    operands = [lists] + pieces
    aliases = {}
    if so_far is not None:
        in_specs.append(pl.BlockSpec(memory_space=pl.ANY))
        aliases = {len(operands): 0}
        operands.append(so_far)
    slots = 4
    scratch = [
        ((copies, blocks * row_count, copies * depth), jnp.bfloat16),
        ((blocks, depth, 2 * BLOCK), jnp.bfloat16),
        ((slots, tiles, parts, row_count, BLOCK), jnp.float32),
    ]
    used = [(value.shape, value.dtype) for value in pieces] + scratch
    vmem_bytes = sum(math.prod(shape) * jnp.dtype(kind).itemsize for shape, kind in used)
    product = tile_total * row_count * 2 * BLOCK
    return pl.pallas_call(
        functools.partial(stack_kernel, (len(whole), len(lows), len(aliases)), freq, scale, pack),
        out_shape=out_shape,
        in_specs=in_specs,
        out_specs=pl.BlockSpec(memory_space=pl.ANY),
        scratch_shapes=[pltpu.VMEM(*spec) for spec in scratch]
        + [pltpu.SMEM(lists.shape, jnp.int32)]
        + [pltpu.SemaphoreType.DMA((slots,)), pltpu.SemaphoreType.DMA],
        input_output_aliases=aliases,
        cost_estimate=pl.CostEstimate(
            flops=2 * product * depth, bytes_accessed=4 * product, transcendentals=0
        ),
        compiler_params=pltpu.CompilerParams(vmem_limit_bytes=vmem_bytes + 8 * 1024 * 1024),
        name="stack",
    )(*operands)


def on_device(spectra, tile_rows, tile_cols):
    window_total = spectra.shape[2] * math.prod(
        lax.axis_size(axis) for axis in ("chip", "core", "col", "win")
    )
    scale = float(1.0 / window_total**0.5)
    slabs = whiten(spectra[0])
    row_count = BLOCK // lax.axis_size("win")
    out_shape = jax.ShapeDtypeStruct(
        (tile_rows.shape[0], len(slabs), 2, row_count, BLOCK), jnp.float32
    )
    lists = by_column(tile_rows, tile_cols)
    block = gather_line(slabs[0])
    arrived, lows, highs = gather_relayed(block)
    whole = [block] + swap_cores([block]) + arrived + swap_cores(arrived)
    lows = lows + swap_cores(lows)
    highs = highs + swap_cores(highs)
    later = [gather_chips(own) for own in slabs[1:]]
    out = stack_bin(0, out_shape, lists, whole, lows, highs, scale, None)
    for freq, rows in enumerate(later, 1):
        rows = lax.optimization_barrier((rows, out))[0]
        out = stack_bin(freq, out_shape, lists, [rows] + swap_cores([rows]), [], [], scale, out)
    return out


def solution(mesh):
    rows, cols, wins = (mesh.shape[axis] for axis in ("row", "col", "win"))
    cores = 2 if rows % 2 == 0 else 1
    mesh = jax.sharding.Mesh(
        mesh.devices.reshape(rows // cores, cores, cols, wins), ("chip", "core", "col", "win")
    )
    devices = ("chip", "core", "col")
    in_specs = (P("win", None, devices, None, None), P(devices), P(devices))
    out_specs = P(devices, None, None, "win", None)
    return jax.shard_map(
        on_device, mesh=mesh, in_specs=in_specs, out_specs=out_specs, check_vma=False
    )
```

```python
import functools
import math

import jax
import jax.numpy as jnp
from jax import lax
from jax.experimental import pallas as pl
from jax.experimental.pallas import tpu as pltpu
from jax.sharding import PartitionSpec as P

BLOCK = 128
MXU = 256


def whiten_kernel(freq, spectra_ref, out_ref):
    freqs = spectra_ref.shape[0]
    power = None
    for at in range(freqs):
        slab = spectra_ref[at]
        term = jnp.sum(slab * slab, axis=1, keepdims=True)
        power = term if power is None else power + term
    factor = jnp.minimum(lax.rsqrt(power / freqs), 1.0)
    out_ref[...] = (spectra_ref[freq] * factor).astype(jnp.bfloat16)


def whiten(spectra, freq):
    _, windows, parts, channels = spectra.shape
    slab = pl.pallas_call(
        functools.partial(whiten_kernel, freq),
        out_shape=jax.ShapeDtypeStruct((windows, parts, channels), jnp.bfloat16),
        name="whiten",
    )(spectra)
    return slab.reshape(windows * parts, channels)


def after(value, *earlier):
    return lax.optimization_barrier((value, *earlier))[0]


def shift(value, axis, step):
    size = lax.axis_size(axis)
    return lax.ppermute(value, axis, [(at, (at + step) % size) for at in range(size)])


def gather_line(own):
    line = [own] + [shift(own, "col", step) for step in range(1, lax.axis_size("col"))]
    return jnp.concatenate(line, axis=0)


def gather_direct(block):
    chips, wins = lax.axis_size("chip"), lax.axis_size("win")
    blocks = []
    for step in range(1, chips * wins):
        chip_step, win_step = step % chips, step // chips
        perm = []
        for chip in range(chips):
            for win in range(wins):
                to = (chip + chip_step) % chips * wins + (win + win_step) % wins
                perm.append((chip * wins + win, to))
        blocks.append(lax.ppermute(block, ("chip", "win"), perm))
    return blocks


def by_column(tile_rows, tile_cols):
    total = tile_rows.shape[0]
    place = jnp.arange(total, dtype=jnp.int32)
    key = tile_cols * total + place
    rank = jnp.sum((key[None, :] < key[:, None]).astype(jnp.int32), axis=1)
    hit = rank[None, :] == place[:, None]
    return jnp.concatenate(
        [
            jnp.sum(jnp.where(hit, values[None, :], 0), axis=1)
            for values in (tile_rows, tile_cols, place)
        ]
    )


def gather_relayed(block):
    half = block.shape[1] // 2
    along_chip = [shift(block, "chip", step) for step in range(1, lax.axis_size("chip"))]
    along_win = [shift(block, "win", step) for step in range(1, lax.axis_size("win"))]
    lows = []
    highs = []
    for chip_step, from_chip in enumerate(along_chip, 1):
        for win_step, from_win in enumerate(along_win, 1):
            lows.append(shift(from_win[:, :half], "chip", chip_step))
            highs.append(shift(from_chip[:, half:], "win", win_step))
    return along_chip + along_win, lows, highs


def swap_cores(values):
    return [shift(value, "core", 1) for value in values] if lax.axis_size("core") == 2 else []


def stack_kernel(counts, freq, scale, pack, lists_hbm, *refs):
    whole_count, half_count, aliased = counts
    whole = refs[:whole_count]
    lows = refs[whole_count : whole_count + half_count]
    piece_count = whole_count + 2 * half_count
    highs = refs[whole_count + half_count : piece_count]
    out_ref, left_ref, right_ref, ring_ref, lists_ref, sems, list_sem = refs[
        piece_count + aliased :
    ]
    total = out_ref.shape[0]
    copies, _, width = left_ref.shape
    depth = right_ref.shape[1]
    slots, tiles, _, row_count, _ = ring_ref.shape
    chunks = pack // copies

    lists = pltpu.make_async_copy(lists_hbm, lists_ref, list_sem)
    lists.start()

    offset = lax.axis_index("win") * row_count
    pick_at = lax.broadcasted_iota(jnp.int32, (2 * row_count, 2 * BLOCK), 0)
    pick_lane = lax.broadcasted_iota(jnp.int32, (2 * row_count, 2 * BLOCK), 1)
    want = pick_at % row_count + offset + pick_at // row_count * BLOCK
    pick = (pick_lane == want).astype(jnp.bfloat16)
    turn_at = lax.broadcasted_iota(jnp.int32, (depth, depth), 0)
    turn_lane = lax.broadcasted_iota(jnp.int32, (depth, depth), 1)
    turn = jnp.where(
        turn_at % 2 == 1,
        jnp.where(turn_lane == turn_at - 1, -1.0, 0.0),
        jnp.where(turn_lane == turn_at + 1, 1.0, 0.0),
    ).astype(jnp.bfloat16)
    place = lax.broadcasted_iota(jnp.int32, (2 * row_count, width), 1) // depth

    def prepare(halves, first, at):
        near = pl.ds(pl.multiple_of((at - first) * 2 * BLOCK, 2 * BLOCK), 2 * BLOCK)
        here = pl.ds(pl.multiple_of(at * 2 * BLOCK, 2 * BLOCK), 2 * BLOCK)
        pieces = [ref[:, here] for ref in whole] + [ref[:, near] for ref in halves]
        rows = jnp.concatenate(pieces, axis=0)
        turned = jnp.dot(turn, rows, preferred_element_type=jnp.float32).astype(jnp.bfloat16)
        left = lax.dot_general(
            pick,
            jnp.concatenate([rows] * copies, axis=0),
            (((1,), (1,)), ((), ())),
            preferred_element_type=jnp.float32,
        )
        where = pl.multiple_of(at * 2 * row_count, 2 * row_count)
        for copy in range(copies):
            only = left if copies == 1 else jnp.where(place == copy, left, 0.0)
            left_ref[copy, pl.ds(where, 2 * row_count), :] = only.astype(jnp.bfloat16)
        for half in range(2):
            lanes = slice(half * BLOCK, (half + 1) * BLOCK)
            right_ref[at * 2 + half, :, :BLOCK] = rows[:, lanes]
            right_ref[at * 2 + half, :, BLOCK:] = turned[:, lanes]

    pairs = whole[0].shape[1] // (2 * BLOCK)
    span = math.gcd(pairs // 2, 8)
    parts = pairs // span

    def prepare_to(done, need):
        def part(halves, first, at, carry):
            for pair in range(span):
                prepare(halves, first, at * span + pair)
            return carry

        if not half_count:
            lax.fori_loop(done, need, functools.partial(part, [], 0), 0)
            return
        middle = parts // 2
        lax.fori_loop(done, jnp.minimum(need, middle), functools.partial(part, lows, 0), 0)
        first = functools.partial(part, highs, middle * span)
        lax.fori_loop(jnp.maximum(done, middle), need, first, 0)

    prepare_to(0, 1)
    lists.wait()

    def send(first, slot, tiles_here):
        for tile in tiles_here:
            to = lists_ref[2 * total + first + tile]
            pltpu.make_async_copy(
                ring_ref.at[slot, tile], out_ref.at[to, freq], sems.at[slot]
            ).start()

    def sent(slot, count):
        pltpu.make_async_copy(
            ring_ref.at[slot, pl.ds(0, count)], out_ref.at[pl.ds(0, count), freq], sems.at[slot]
        ).wait()

    def compute(first, slot, count, between):
        for group in range(count // pack):
            lefts = []
            rights = []
            for member in range(pack):
                at = first + group * pack + member
                left_at = pl.multiple_of(lists_ref[at] * row_count, row_count)
                left = left_ref[member % copies, pl.ds(left_at, row_count), :]
                if chunks > 1:
                    chunk = member // copies
                    empty = jnp.zeros_like(left)
                    left = jnp.concatenate(
                        [left if spot == chunk else empty for spot in range(chunks)], axis=1
                    )
                lefts.append(left)
                rights.append(right_ref[lists_ref[total + at]])
            product = jnp.dot(
                jnp.concatenate(lefts, axis=0),
                jnp.concatenate(rights, axis=0),
                preferred_element_type=jnp.float32,
            )
            product = product * scale
            for member in range(pack):
                mine = product[member * row_count : (member + 1) * row_count]
                ring_ref[slot, group * pack + member, 0] = mine[:, :BLOCK]
                ring_ref[slot, group * pack + member, 1] = mine[:, BLOCK:]
            between(group)

    def needed(last):
        return lists_ref[total + last] // (2 * span) + 1

    start = total % tiles or tiles
    steps = (total - start) // tiles
    groups = tiles // pack

    def first_of(step):
        return start + (step - 1) * tiles

    done = jnp.maximum(needed(start - 1), 1)
    prepare_to(1, done)
    compute(0, 0, start, lambda group: None)
    send(0, 0, range(start))

    def stack(step, done, opening):
        first = first_of(step)
        slot = lax.rem(step, slots)
        before = lax.rem(step + slots - 1, slots)
        need = jnp.maximum(needed(first + tiles - 1), done)
        prepare_to(done, need)

        @pl.when(step > slots)
        def _():
            sent(slot, tiles)

        if opening:
            compute(first, slot, tiles, lambda group: None)
            return need

        @pl.when(step == slots)
        def _():
            sent(slot, start)

        def between(group):
            send(first - tiles, before, range(group * pack, (group + 1) * pack))

        compute(first, slot, tiles, between)
        return need

    if steps:
        done = stack(1, done, True)
        lax.fori_loop(2, steps + 1, lambda step, done: stack(step, done, False), done)
        send(first_of(steps), steps % slots, range(tiles))
    flying = [(step % slots, tiles if step else start) for step in range(steps + 1)]
    for slot, count in flying[-slots:]:
        sent(slot, count)


def stack_bin(freq, out_shape, lists, whole, lows, highs, scale, so_far):
    pieces = whole + lows + highs
    channels = whole[0].shape[1]
    depth = sum(value.shape[0] for value in whole + lows)
    tile_total, _, parts, row_count, _ = out_shape.shape
    pack = math.gcd(tile_total, max(1, MXU // depth))
    copies = min(pack, max(1, BLOCK // depth))
    tiles = max(pack, 24 // pack * pack)
    tiles = min(tiles, tile_total)
    blocks = channels // BLOCK
    vmem = pl.BlockSpec(memory_space=pltpu.VMEM)
    in_specs = [pl.BlockSpec(memory_space=pl.ANY)] + [vmem] * len(pieces)
    operands = [lists] + pieces
    aliases = {}
    if so_far is not None:
        in_specs.append(pl.BlockSpec(memory_space=pl.ANY))
        aliases = {len(operands): 0}
        operands.append(so_far)
    slots = 4
    scratch = [
        ((copies, blocks * row_count, copies * depth), jnp.bfloat16),
        ((blocks, depth, 2 * BLOCK), jnp.bfloat16),
        ((slots, tiles, parts, row_count, BLOCK), jnp.float32),
    ]
    used = [(value.shape, value.dtype) for value in pieces] + scratch
    vmem_bytes = sum(math.prod(shape) * jnp.dtype(kind).itemsize for shape, kind in used)
    return pl.pallas_call(
        functools.partial(stack_kernel, (len(whole), len(lows), len(aliases)), freq, scale, pack),
        out_shape=out_shape,
        in_specs=in_specs,
        out_specs=pl.BlockSpec(memory_space=pl.ANY),
        scratch_shapes=[pltpu.VMEM(*spec) for spec in scratch]
        + [pltpu.SMEM(lists.shape, jnp.int32)]
        + [pltpu.SemaphoreType.DMA((slots,)), pltpu.SemaphoreType.DMA],
        input_output_aliases=aliases,
        cost_estimate=pl.CostEstimate(flops=0, bytes_accessed=0, transcendentals=0),
        compiler_params=pltpu.CompilerParams(vmem_limit_bytes=vmem_bytes + 8 * 1024 * 1024),
        name="stack",
    )(*operands)


def on_device(spectra, tile_rows, tile_cols):
    window_total = spectra.shape[2] * math.prod(
        lax.axis_size(axis) for axis in ("chip", "core", "col", "win")
    )
    scale = float(1.0 / window_total**0.5)
    freqs = spectra.shape[1]
    row_count = BLOCK // lax.axis_size("win")
    out_shape = jax.ShapeDtypeStruct(
        (tile_rows.shape[0], freqs, 2, row_count, BLOCK), jnp.float32
    )
    lists = by_column(tile_rows, tile_cols)
    block = gather_line(whiten(spectra[0], 0))
    swapped = swap_cores([block])
    arrived, lows, highs = gather_relayed(block)
    whole = [block] + swapped + arrived + swap_cores(arrived)
    lows = lows + swap_cores(lows)
    highs = highs + swap_cores(highs)
    later = []
    for freq in range(1, freqs):
        own = after(whiten(spectra[0], freq), *swapped)
        block = gather_line(own)
        swapped = swap_cores([block])
        arrived = gather_direct(after(block, *arrived))
        later.append(([block] + swapped, arrived))
    out = stack_bin(0, out_shape, lists, whole, lows, highs, scale, None)
    for freq, (whole, arrived) in enumerate(later, 1):
        arrived = list(after(tuple(arrived), out))
        whole = whole + arrived + swap_cores(arrived)
        out = stack_bin(freq, out_shape, lists, whole, [], [], scale, out)
    return out


def solution(mesh):
    rows, cols, wins = (mesh.shape[axis] for axis in ("row", "col", "win"))
    cores = 2 if rows % 2 == 0 else 1
    mesh = jax.sharding.Mesh(
        mesh.devices.reshape(rows // cores, cores, cols, wins), ("chip", "core", "col", "win")
    )
    devices = ("chip", "core", "col")
    in_specs = (P("win", None, devices, None, None), P(devices), P(devices))
    out_specs = P(devices, None, None, "win", None)
    return jax.shard_map(
        on_device, mesh=mesh, in_specs=in_specs, out_specs=out_specs, check_vma=False
    )
```

```python
import functools
import math

import jax
import jax.numpy as jnp
from jax import lax
from jax.experimental import pallas as pl
from jax.experimental.pallas import tpu as pltpu
from jax.sharding import PartitionSpec as P

BLOCK = 128
MXU = 256


def whiten_kernel(spectra_ref, *out_refs):
    freqs = spectra_ref.shape[0]
    power = None
    for freq in range(freqs):
        slab = spectra_ref[freq]
        term = jnp.sum(slab * slab, axis=1, keepdims=True)
        power = term if power is None else power + term
    factor = jnp.minimum(lax.rsqrt(power / freqs), 1.0)
    for freq in range(freqs):
        out_refs[freq][...] = (spectra_ref[freq] * factor).astype(jnp.bfloat16)


def whiten(spectra):
    freqs, windows, parts, channels = spectra.shape
    shape = jax.ShapeDtypeStruct((windows, parts, channels), jnp.bfloat16)
    slabs = pl.pallas_call(whiten_kernel, out_shape=[shape] * freqs, name="whiten")(spectra)
    return [slab.reshape(windows * parts, channels) for slab in slabs]


def after(value, *earlier):
    return lax.optimization_barrier((value, *earlier))[0]


def shift(value, axis, step):
    size = lax.axis_size(axis)
    return lax.ppermute(value, axis, [(at, (at + step) % size) for at in range(size)])


def gather_line(own):
    line = [own] + [shift(own, "col", step) for step in range(1, lax.axis_size("col"))]
    return jnp.concatenate(line, axis=0)


def gather_direct(block, near, far):
    chips, wins = lax.axis_size("chip"), lax.axis_size("win")
    blocks = []
    for step in range(1, chips * wins):
        chip_step, win_step = step % chips, step // chips
        perm = []
        for chip in range(chips):
            for win in range(wins):
                to = (chip + chip_step) % chips * wins + (win + win_step) % wins
                perm.append((chip * wins + win, to))
        sent = after(block, *(far if chip_step and win_step else near))
        blocks.append(lax.ppermute(sent, ("chip", "win"), perm))
    return blocks


def by_column(tile_rows, tile_cols):
    total = tile_rows.shape[0]
    place = jnp.arange(total, dtype=jnp.int32)
    key = tile_cols * total + place
    rank = jnp.sum((key[None, :] < key[:, None]).astype(jnp.int32), axis=1)
    hit = rank[None, :] == place[:, None]
    return jnp.concatenate(
        [
            jnp.sum(jnp.where(hit, values[None, :], 0), axis=1)
            for values in (tile_rows, tile_cols, place)
        ]
    )


def gather_relayed(block):
    half = block.shape[1] // 2
    along_chip = [shift(block, "chip", step) for step in range(1, lax.axis_size("chip"))]
    along_win = [shift(block, "win", step) for step in range(1, lax.axis_size("win"))]
    lows = []
    highs = []
    for chip_step, from_chip in enumerate(along_chip, 1):
        for win_step, from_win in enumerate(along_win, 1):
            lows.append(shift(from_win[:, :half], "chip", chip_step))
            highs.append(shift(from_chip[:, half:], "win", win_step))
    return along_chip + along_win, lows, highs


def swap_cores(values):
    return [shift(value, "core", 1) for value in values] if lax.axis_size("core") == 2 else []


def stack_kernel(counts, freq, scale, pack, lists_hbm, *refs):
    whole_count, half_count, aliased = counts
    whole = refs[:whole_count]
    lows = refs[whole_count : whole_count + half_count]
    piece_count = whole_count + 2 * half_count
    highs = refs[whole_count + half_count : piece_count]
    out_ref, left_ref, right_ref, ring_ref, lists_ref, sems, list_sem = refs[
        piece_count + aliased :
    ]
    total = out_ref.shape[0]
    copies, _, width = left_ref.shape
    depth = right_ref.shape[1]
    slots, tiles, _, row_count, _ = ring_ref.shape
    chunks = pack // copies

    lists = pltpu.make_async_copy(lists_hbm, lists_ref, list_sem)
    lists.start()

    offset = lax.axis_index("win") * row_count
    pick_at = lax.broadcasted_iota(jnp.int32, (2 * row_count, 2 * BLOCK), 0)
    pick_lane = lax.broadcasted_iota(jnp.int32, (2 * row_count, 2 * BLOCK), 1)
    want = pick_at % row_count + offset + pick_at // row_count * BLOCK
    pick = (pick_lane == want).astype(jnp.bfloat16)
    turn_at = lax.broadcasted_iota(jnp.int32, (depth, depth), 0)
    turn_lane = lax.broadcasted_iota(jnp.int32, (depth, depth), 1)
    turn = jnp.where(
        turn_at % 2 == 1,
        jnp.where(turn_lane == turn_at - 1, -1.0, 0.0),
        jnp.where(turn_lane == turn_at + 1, 1.0, 0.0),
    ).astype(jnp.bfloat16)
    place = lax.broadcasted_iota(jnp.int32, (2 * row_count, width), 1) // depth

    def prepare(halves, first, at):
        near = pl.ds(pl.multiple_of((at - first) * 2 * BLOCK, 2 * BLOCK), 2 * BLOCK)
        here = pl.ds(pl.multiple_of(at * 2 * BLOCK, 2 * BLOCK), 2 * BLOCK)
        pieces = [ref[:, here] for ref in whole] + [ref[:, near] for ref in halves]
        rows = jnp.concatenate(pieces, axis=0)
        turned = jnp.dot(turn, rows, preferred_element_type=jnp.float32).astype(jnp.bfloat16)
        left = lax.dot_general(
            pick,
            jnp.concatenate([rows] * copies, axis=0),
            (((1,), (1,)), ((), ())),
            preferred_element_type=jnp.float32,
        )
        where = pl.multiple_of(at * 2 * row_count, 2 * row_count)
        for copy in range(copies):
            only = left if copies == 1 else jnp.where(place == copy, left, 0.0)
            left_ref[copy, pl.ds(where, 2 * row_count), :] = only.astype(jnp.bfloat16)
        for half in range(2):
            lanes = slice(half * BLOCK, (half + 1) * BLOCK)
            right_ref[at * 2 + half, :, :BLOCK] = rows[:, lanes]
            right_ref[at * 2 + half, :, BLOCK:] = turned[:, lanes]

    pairs = whole[0].shape[1] // (2 * BLOCK)
    span = math.gcd(pairs // 2, 8)
    parts = pairs // span

    def prepare_to(done, need):
        def part(halves, first, at, carry):
            for pair in range(span):
                prepare(halves, first, at * span + pair)
            return carry

        if not half_count:
            lax.fori_loop(done, need, functools.partial(part, [], 0), 0)
            return
        middle = parts // 2
        lax.fori_loop(done, jnp.minimum(need, middle), functools.partial(part, lows, 0), 0)
        first = functools.partial(part, highs, middle * span)
        lax.fori_loop(jnp.maximum(done, middle), need, first, 0)

    prepare_to(0, 1)
    lists.wait()

    def send(first, slot, tiles_here):
        for tile in tiles_here:
            to = lists_ref[2 * total + first + tile]
            pltpu.make_async_copy(
                ring_ref.at[slot, tile], out_ref.at[to, freq], sems.at[slot]
            ).start()

    def sent(slot, count):
        pltpu.make_async_copy(
            ring_ref.at[slot, pl.ds(0, count)], out_ref.at[pl.ds(0, count), freq], sems.at[slot]
        ).wait()

    def compute(first, slot, count):
        for group in range(count // pack):
            lefts = []
            rights = []
            for member in range(pack):
                at = first + group * pack + member
                left_at = pl.multiple_of(lists_ref[at] * row_count, row_count)
                left = left_ref[member % copies, pl.ds(left_at, row_count), :]
                if chunks > 1:
                    chunk = member // copies
                    empty = jnp.zeros_like(left)
                    left = jnp.concatenate(
                        [left if spot == chunk else empty for spot in range(chunks)], axis=1
                    )
                lefts.append(left)
                rights.append(right_ref[lists_ref[total + at]])
            product = jnp.dot(
                jnp.concatenate(lefts, axis=0),
                jnp.concatenate(rights, axis=0),
                preferred_element_type=jnp.float32,
            )
            product = product * scale
            for member in range(pack):
                mine = product[member * row_count : (member + 1) * row_count]
                ring_ref[slot, group * pack + member, 0] = mine[:, :BLOCK]
                ring_ref[slot, group * pack + member, 1] = mine[:, BLOCK:]

    def needed(last):
        return lists_ref[total + last] // (2 * span) + 1

    steps = total // tiles
    rest = total % tiles

    def stack(step, done):
        first = step * tiles
        slot = lax.rem(step, slots)
        need = jnp.maximum(needed(first + tiles - 1), done)
        prepare_to(done, need)

        @pl.when(step >= slots)
        def _():
            sent(slot, tiles)

        compute(first, slot, tiles)
        send(first, slot, range(tiles))
        return need

    done = lax.fori_loop(0, steps, stack, jnp.int32(1))
    flying = [(step % slots, tiles) for step in range(steps)][-slots:]
    if rest:
        prepare_to(done, needed(total - 1))
        slot = steps % slots
        if steps >= slots:
            sent(slot, tiles)
            flying = flying[1:]
        compute(steps * tiles, slot, rest)
        send(steps * tiles, slot, range(rest))
        flying.append((slot, rest))
    for slot, count in flying:
        sent(slot, count)


def stack_bin(freq, out_shape, lists, whole, lows, highs, scale, so_far):
    pieces = whole + lows + highs
    channels = whole[0].shape[1]
    depth = sum(value.shape[0] for value in whole + lows)
    tile_total, _, parts, row_count, _ = out_shape.shape
    pack = math.gcd(tile_total, max(1, MXU // depth))
    copies = min(pack, max(1, BLOCK // depth))
    tiles = max(pack, 24 // pack * pack)
    tiles = min(tiles, tile_total)
    blocks = channels // BLOCK
    vmem = pl.BlockSpec(memory_space=pltpu.VMEM)
    in_specs = [pl.BlockSpec(memory_space=pl.ANY)] + [vmem] * len(pieces)
    operands = [lists] + pieces
    aliases = {}
    if so_far is not None:
        in_specs.append(pl.BlockSpec(memory_space=pl.ANY))
        aliases = {len(operands): 0}
        operands.append(so_far)
    slots = 4
    scratch = [
        ((copies, blocks * row_count, copies * depth), jnp.bfloat16),
        ((blocks, depth, 2 * BLOCK), jnp.bfloat16),
        ((slots, tiles, parts, row_count, BLOCK), jnp.float32),
    ]
    used = [(value.shape, value.dtype) for value in pieces] + scratch
    vmem_bytes = sum(math.prod(shape) * jnp.dtype(kind).itemsize for shape, kind in used)
    return pl.pallas_call(
        functools.partial(stack_kernel, (len(whole), len(lows), len(aliases)), freq, scale, pack),
        out_shape=out_shape,
        in_specs=in_specs,
        out_specs=pl.BlockSpec(memory_space=pl.ANY),
        scratch_shapes=[pltpu.VMEM(*spec) for spec in scratch]
        + [pltpu.SMEM(lists.shape, jnp.int32)]
        + [pltpu.SemaphoreType.DMA((slots,)), pltpu.SemaphoreType.DMA],
        input_output_aliases=aliases,
        cost_estimate=pl.CostEstimate(flops=0, bytes_accessed=0, transcendentals=0),
        compiler_params=pltpu.CompilerParams(vmem_limit_bytes=vmem_bytes + 8 * 1024 * 1024),
        name="stack",
    )(*operands)


def on_device(spectra, tile_rows, tile_cols):
    window_total = spectra.shape[2] * math.prod(
        lax.axis_size(axis) for axis in ("chip", "core", "col", "win")
    )
    scale = float(1.0 / window_total**0.5)
    freqs = spectra.shape[1]
    row_count = BLOCK // lax.axis_size("win")
    out_shape = jax.ShapeDtypeStruct(
        (tile_rows.shape[0], freqs, 2, row_count, BLOCK), jnp.float32
    )
    lists = by_column(tile_rows, tile_cols)
    slabs = whiten(spectra[0])
    block = gather_line(slabs[0])
    block, lists = lax.optimization_barrier((block, lists))
    swapped = swap_cores([block])
    arrived, lows, highs = gather_relayed(block)
    near, far = arrived, lows + highs
    whole = [block] + swapped + arrived + swap_cores(arrived)
    lows = lows + swap_cores(lows)
    highs = highs + swap_cores(highs)
    later = []
    for own in slabs[1:]:
        block = gather_line(after(own, *swapped))
        swapped = swap_cores([block])
        arrived = gather_direct(block, near, far)
        near, far = arrived, arrived
        later.append(([block] + swapped, arrived))
    out = stack_bin(0, out_shape, lists, whole, lows, highs, scale, None)
    for freq, (whole, arrived) in enumerate(later, 1):
        arrived = list(after(tuple(arrived), out))
        whole = whole + arrived + swap_cores(arrived)
        out = stack_bin(freq, out_shape, lists, whole, [], [], scale, out)
    return out


def solution(mesh):
    rows, cols, wins = (mesh.shape[axis] for axis in ("row", "col", "win"))
    cores = 2 if rows % 2 == 0 else 1
    mesh = jax.sharding.Mesh(
        mesh.devices.reshape(rows // cores, cores, cols, wins), ("chip", "core", "col", "win")
    )
    devices = ("chip", "core", "col")
    in_specs = (P("win", None, devices, None, None), P(devices), P(devices))
    out_specs = P(devices, None, None, "win", None)
    return jax.shard_map(
        on_device, mesh=mesh, in_specs=in_specs, out_specs=out_specs, check_vma=False
    )
```

```python
import functools
import math

import jax
import jax.numpy as jnp
from jax import lax
from jax.experimental import pallas as pl
from jax.experimental.pallas import tpu as pltpu
from jax.sharding import PartitionSpec as P

BLOCK = 128
MXU = 256


def whiten_kernel(spectra_ref, *out_refs):
    freqs = spectra_ref.shape[0]
    power = None
    for freq in range(freqs):
        for part in range(2):
            row = spectra_ref[freq, :, part : part + 1, :]
            power = row * row if power is None else power + row * row
    factor = jnp.minimum(lax.rsqrt(power / freqs), 1.0)
    for freq in range(freqs):
        out_refs[freq][...] = (spectra_ref[freq] * factor).astype(jnp.bfloat16)


def whiten(spectra):
    freqs, windows, parts, channels = spectra.shape
    shape = jax.ShapeDtypeStruct((windows, parts, channels), jnp.bfloat16)
    slabs = pl.pallas_call(whiten_kernel, out_shape=[shape] * freqs, name="whiten")(spectra)
    return [slab.reshape(windows * parts, channels) for slab in slabs]


def after(value, *earlier):
    return lax.optimization_barrier((value, *earlier))[0]


def shift(value, axis, step):
    size = lax.axis_size(axis)
    return lax.ppermute(value, axis, [(at, (at + step) % size) for at in range(size)])


def join_kernel(*refs):
    refs[-1][...] = jnp.concatenate([ref[...] for ref in refs[:-1]], axis=0)


def gather_line(own, first):
    line = [own] + [shift(own, "col", step) for step in range(1, lax.axis_size("col"))]
    if not first:
        return jnp.concatenate(line, axis=0)
    shape = (len(line) * own.shape[0], own.shape[1])
    return pl.pallas_call(
        join_kernel,
        out_shape=jax.ShapeDtypeStruct(shape, own.dtype),
        name="join",
    )(*line)


def gather_direct(block, near, far):
    chips, wins = lax.axis_size("chip"), lax.axis_size("win")
    blocks = []
    for step in range(1, chips * wins):
        chip_step, win_step = step % chips, step // chips
        perm = []
        for chip in range(chips):
            for win in range(wins):
                to = (chip + chip_step) % chips * wins + (win + win_step) % wins
                perm.append((chip * wins + win, to))
        sent = after(block, *(far if chip_step and win_step else near))
        blocks.append(lax.ppermute(sent, ("chip", "win"), perm))
    return blocks


def by_column(tile_rows, tile_cols):
    total = tile_rows.shape[0]
    place = jnp.arange(total, dtype=jnp.int32)
    key = tile_cols * total + place
    rank = jnp.sum((key[None, :] < key[:, None]).astype(jnp.int32), axis=1)
    hit = rank[None, :] == place[:, None]
    return jnp.concatenate(
        [
            jnp.sum(jnp.where(hit, values[None, :], 0), axis=1)
            for values in (tile_rows, tile_cols, place)
        ]
    )


def gather_relayed(block):
    half = block.shape[1] // 2
    along_chip = [shift(block, "chip", step) for step in range(1, lax.axis_size("chip"))]
    along_win = [shift(block, "win", step) for step in range(1, lax.axis_size("win"))]
    lows = []
    highs = []
    for chip_step, from_chip in enumerate(along_chip, 1):
        for win_step, from_win in enumerate(along_win, 1):
            lows.append(shift(from_win[:, :half], "chip", chip_step))
            highs.append(shift(from_chip[:, half:], "win", win_step))
    return along_chip + along_win, lows, highs


def swap_cores(values):
    return [shift(value, "core", 1) for value in values] if lax.axis_size("core") == 2 else []


def stack_kernel(counts, freq, scale, pack, lists_hbm, *refs):
    whole_count, half_count, aliased = counts
    whole = refs[:whole_count]
    lows = refs[whole_count : whole_count + half_count]
    piece_count = whole_count + 2 * half_count
    highs = refs[whole_count + half_count : piece_count]
    out_ref, left_ref, right_ref, ring_ref, lists_ref, sems, list_sem = refs[
        piece_count + aliased :
    ]
    total = out_ref.shape[0]
    copies, _, width = left_ref.shape
    depth = right_ref.shape[1]
    slots, tiles, _, row_count, _ = ring_ref.shape
    chunks = pack // copies

    lists = pltpu.make_async_copy(lists_hbm, lists_ref, list_sem)
    lists.start()

    offset = lax.axis_index("win") * row_count
    pick_at = lax.broadcasted_iota(jnp.int32, (2 * row_count, 2 * BLOCK), 0)
    pick_lane = lax.broadcasted_iota(jnp.int32, (2 * row_count, 2 * BLOCK), 1)
    want = pick_at % row_count + offset + pick_at // row_count * BLOCK
    pick = (pick_lane == want).astype(jnp.bfloat16)
    turn_at = lax.broadcasted_iota(jnp.int32, (depth, depth), 0)
    turn_lane = lax.broadcasted_iota(jnp.int32, (depth, depth), 1)
    turn = jnp.where(
        turn_at % 2 == 1,
        jnp.where(turn_lane == turn_at - 1, -1.0, 0.0),
        jnp.where(turn_lane == turn_at + 1, 1.0, 0.0),
    ).astype(jnp.bfloat16)
    place = lax.broadcasted_iota(jnp.int32, (2 * row_count, width), 1) // depth

    def prepare(halves, first, at):
        near = pl.ds(pl.multiple_of((at - first) * 2 * BLOCK, 2 * BLOCK), 2 * BLOCK)
        here = pl.ds(pl.multiple_of(at * 2 * BLOCK, 2 * BLOCK), 2 * BLOCK)
        pieces = [ref[:, here] for ref in whole] + [ref[:, near] for ref in halves]
        rows = jnp.concatenate(pieces, axis=0)
        turned = jnp.dot(turn, rows, preferred_element_type=jnp.float32).astype(jnp.bfloat16)
        left = lax.dot_general(
            pick,
            jnp.concatenate([rows] * copies, axis=0),
            (((1,), (1,)), ((), ())),
            preferred_element_type=jnp.float32,
        )
        where = pl.multiple_of(at * 2 * row_count, 2 * row_count)
        for copy in range(copies):
            only = left if copies == 1 else jnp.where(place == copy, left, 0.0)
            left_ref[copy, pl.ds(where, 2 * row_count), :] = only.astype(jnp.bfloat16)
        for half in range(2):
            lanes = slice(half * BLOCK, (half + 1) * BLOCK)
            right_ref[at * 2 + half, :, :BLOCK] = rows[:, lanes]
            right_ref[at * 2 + half, :, BLOCK:] = turned[:, lanes]

    pairs = whole[0].shape[1] // (2 * BLOCK)
    span = math.gcd(pairs // 2, 8)
    parts = pairs // span

    def prepare_to(done, need):
        def part(halves, first, at, carry):
            for pair in range(span):
                prepare(halves, first, at * span + pair)
            return carry

        if not half_count:
            lax.fori_loop(done, need, functools.partial(part, [], 0), 0)
            return
        middle = parts // 2
        lax.fori_loop(done, jnp.minimum(need, middle), functools.partial(part, lows, 0), 0)
        first = functools.partial(part, highs, middle * span)
        lax.fori_loop(jnp.maximum(done, middle), need, first, 0)

    prepare_to(0, 1)
    lists.wait()

    def send(first, slot, tiles_here):
        for tile in tiles_here:
            to = lists_ref[2 * total + first + tile]
            pltpu.make_async_copy(
                ring_ref.at[slot, tile], out_ref.at[to, freq], sems.at[slot]
            ).start()

    def sent(slot, count):
        pltpu.make_async_copy(
            ring_ref.at[slot, pl.ds(0, count)], out_ref.at[pl.ds(0, count), freq], sems.at[slot]
        ).wait()

    def compute(first, slot, count):
        for group in range(count // pack):
            lefts = []
            rights = []
            for member in range(pack):
                at = first + group * pack + member
                left_at = pl.multiple_of(lists_ref[at] * row_count, row_count)
                left = left_ref[member % copies, pl.ds(left_at, row_count), :]
                if chunks > 1:
                    chunk = member // copies
                    empty = jnp.zeros_like(left)
                    left = jnp.concatenate(
                        [left if spot == chunk else empty for spot in range(chunks)], axis=1
                    )
                lefts.append(left)
                rights.append(right_ref[lists_ref[total + at]])
            product = jnp.dot(
                jnp.concatenate(lefts, axis=0),
                jnp.concatenate(rights, axis=0),
                preferred_element_type=jnp.float32,
            )
            product = product * scale
            for member in range(pack):
                mine = product[member * row_count : (member + 1) * row_count]
                ring_ref[slot, group * pack + member, 0] = mine[:, :BLOCK]
                ring_ref[slot, group * pack + member, 1] = mine[:, BLOCK:]

    def needed(last):
        return lists_ref[total + last] // (2 * span) + 1

    steps = total // tiles
    rest = total % tiles

    def stack(step, done):
        first = step * tiles
        slot = lax.rem(step, slots)
        need = jnp.maximum(needed(first + tiles - 1), done)
        prepare_to(done, need)

        @pl.when(step >= slots)
        def _():
            sent(slot, tiles)

        compute(first, slot, tiles)
        send(first, slot, range(tiles))
        return need

    done = lax.fori_loop(0, steps, stack, jnp.int32(1))
    flying = [(step % slots, tiles) for step in range(steps)][-slots:]
    if rest:
        prepare_to(done, needed(total - 1))
        slot = steps % slots
        if steps >= slots:
            sent(slot, tiles)
            flying = flying[1:]
        compute(steps * tiles, slot, rest)
        send(steps * tiles, slot, range(rest))
        flying.append((slot, rest))
    for slot, count in flying:
        sent(slot, count)


def stack_bin(freq, out_shape, lists, whole, lows, highs, scale, so_far):
    pieces = whole + lows + highs
    channels = whole[0].shape[1]
    depth = sum(value.shape[0] for value in whole + lows)
    tile_total, _, parts, row_count, _ = out_shape.shape
    pack = math.gcd(tile_total, max(1, MXU // depth))
    copies = min(pack, max(1, BLOCK // depth))
    tiles = max(pack, 24 // pack * pack)
    tiles = min(tiles, tile_total)
    blocks = channels // BLOCK
    vmem = pl.BlockSpec(memory_space=pltpu.VMEM)
    in_specs = [pl.BlockSpec(memory_space=pl.ANY)] + [vmem] * len(pieces)
    operands = [lists] + pieces
    aliases = {}
    if so_far is not None:
        in_specs.append(pl.BlockSpec(memory_space=pl.ANY))
        aliases = {len(operands): 0}
        operands.append(so_far)
    slots = 4
    scratch = [
        ((copies, blocks * row_count, copies * depth), jnp.bfloat16),
        ((blocks, depth, 2 * BLOCK), jnp.bfloat16),
        ((slots, tiles, parts, row_count, BLOCK), jnp.float32),
    ]
    used = [(value.shape, value.dtype) for value in pieces] + scratch
    vmem_bytes = sum(math.prod(shape) * jnp.dtype(kind).itemsize for shape, kind in used)
    return pl.pallas_call(
        functools.partial(stack_kernel, (len(whole), len(lows), len(aliases)), freq, scale, pack),
        out_shape=out_shape,
        in_specs=in_specs,
        out_specs=pl.BlockSpec(memory_space=pl.ANY),
        scratch_shapes=[pltpu.VMEM(*spec) for spec in scratch]
        + [pltpu.SMEM(lists.shape, jnp.int32)]
        + [pltpu.SemaphoreType.DMA((slots,)), pltpu.SemaphoreType.DMA],
        input_output_aliases=aliases,
        cost_estimate=pl.CostEstimate(flops=0, bytes_accessed=0, transcendentals=0),
        compiler_params=pltpu.CompilerParams(vmem_limit_bytes=vmem_bytes + 8 * 1024 * 1024),
        name="stack",
    )(*operands)


def on_device(spectra, tile_rows, tile_cols):
    window_total = spectra.shape[2] * math.prod(
        lax.axis_size(axis) for axis in ("chip", "core", "col", "win")
    )
    scale = float(1.0 / window_total**0.5)
    freqs = spectra.shape[1]
    row_count = BLOCK // lax.axis_size("win")
    out_shape = jax.ShapeDtypeStruct(
        (tile_rows.shape[0], freqs, 2, row_count, BLOCK), jnp.float32
    )
    lists = by_column(tile_rows, tile_cols)
    slabs = whiten(spectra[0])
    block = gather_line(slabs[0], True)
    block, lists = lax.optimization_barrier((block, lists))
    swapped = swap_cores([block])
    arrived, lows, highs = gather_relayed(block)
    near, far = arrived, lows + highs
    whole = [block] + swapped + arrived + swap_cores(arrived)
    lows = lows + swap_cores(lows)
    highs = highs + swap_cores(highs)
    later = []
    for own in slabs[1:]:
        block = gather_line(after(own, *swapped), False)
        swapped = swap_cores([block])
        arrived = gather_direct(block, near, far)
        near, far = arrived, arrived
        later.append(([block] + swapped, arrived))
    out = stack_bin(0, out_shape, lists, whole, lows, highs, scale, None)
    for freq, (whole, arrived) in enumerate(later, 1):
        arrived = list(after(tuple(arrived), out))
        whole = whole + arrived + swap_cores(arrived)
        out = stack_bin(freq, out_shape, lists, whole, [], [], scale, out)
    return out


def solution(mesh):
    rows, cols, wins = (mesh.shape[axis] for axis in ("row", "col", "win"))
    cores = 2 if rows % 2 == 0 else 1
    mesh = jax.sharding.Mesh(
        mesh.devices.reshape(rows // cores, cores, cols, wins), ("chip", "core", "col", "win")
    )
    devices = ("chip", "core", "col")
    in_specs = (P("win", None, devices, None, None), P(devices), P(devices))
    out_specs = P(devices, None, None, "win", None)
    return jax.shard_map(
        on_device, mesh=mesh, in_specs=in_specs, out_specs=out_specs, check_vma=False
    )
```

```python
import functools
import math

import jax
import jax.numpy as jnp
from jax import lax
from jax.experimental import pallas as pl
from jax.experimental.pallas import tpu as pltpu
from jax.sharding import PartitionSpec as P

BLOCK = 128
MXU = 256


def whiten_kernel(spectra_ref, *out_refs):
    freqs = spectra_ref.shape[0]
    power = None
    for freq in range(freqs):
        for part in range(2):
            row = spectra_ref[freq, :, part : part + 1, :]
            power = row * row if power is None else power + row * row
    factor = jnp.minimum(lax.rsqrt(power / freqs), 1.0)
    for freq in range(freqs):
        out_refs[freq][...] = (spectra_ref[freq] * factor).astype(jnp.bfloat16)


def whiten(spectra):
    freqs, windows, parts, channels = spectra.shape
    shape = jax.ShapeDtypeStruct((windows, parts, channels), jnp.bfloat16)
    slabs = pl.pallas_call(whiten_kernel, out_shape=[shape] * freqs, name="whiten")(spectra)
    return [slab.reshape(windows * parts, channels) for slab in slabs]


def after(value, *earlier):
    return lax.optimization_barrier((value, *earlier))[0]


def shift(value, axis, step):
    size = lax.axis_size(axis)
    return lax.ppermute(value, axis, [(at, (at + step) % size) for at in range(size)])


def gather_line(own):
    line = [own] + [shift(own, "col", step) for step in range(1, lax.axis_size("col"))]
    return jnp.concatenate(line, axis=0)


def gather_direct(block, near, far):
    chips, wins = lax.axis_size("chip"), lax.axis_size("win")
    blocks = []
    for step in range(1, chips * wins):
        chip_step, win_step = step % chips, step // chips
        perm = []
        for chip in range(chips):
            for win in range(wins):
                to = (chip + chip_step) % chips * wins + (win + win_step) % wins
                perm.append((chip * wins + win, to))
        sent = after(block, *(far if chip_step and win_step else near))
        blocks.append(lax.ppermute(sent, ("chip", "win"), perm))
    return blocks


def by_column(tile_rows, tile_cols):
    total = tile_rows.shape[0]
    place = jnp.arange(total, dtype=jnp.int32)
    key = tile_cols * total + place
    rank = jnp.sum((key[None, :] < key[:, None]).astype(jnp.int32), axis=1)
    hit = rank[None, :] == place[:, None]
    return jnp.concatenate(
        [
            jnp.sum(jnp.where(hit, values[None, :], 0), axis=1)
            for values in (tile_rows, tile_cols, place)
        ]
    )


def gather_relayed(block):
    half = block.shape[1] // 2
    along_chip = [shift(block, "chip", step) for step in range(1, lax.axis_size("chip"))]
    along_win = [shift(block, "win", step) for step in range(1, lax.axis_size("win"))]
    lows = []
    highs = []
    for chip_step, from_chip in enumerate(along_chip, 1):
        for win_step, from_win in enumerate(along_win, 1):
            lows.append(shift(from_win[:, :half], "chip", chip_step))
            highs.append(shift(from_chip[:, half:], "win", win_step))
    return along_chip + along_win, lows, highs


def swap_cores(values):
    return [shift(value, "core", 1) for value in values] if lax.axis_size("core") == 2 else []


def stack_kernel(counts, freq, scale, pack, lists_hbm, *refs):
    whole_count, half_count, aliased = counts
    whole = refs[:whole_count]
    lows = refs[whole_count : whole_count + half_count]
    piece_count = whole_count + 2 * half_count
    highs = refs[whole_count + half_count : piece_count]
    out_ref, left_ref, right_ref, ring_ref, lists_ref, sems, list_sem = refs[
        piece_count + aliased :
    ]
    total = out_ref.shape[0]
    copies, _, width = left_ref.shape
    depth = right_ref.shape[1]
    slots, tiles, _, row_count, _ = ring_ref.shape
    chunks = pack // copies

    lists = pltpu.make_async_copy(lists_hbm, lists_ref, list_sem)
    lists.start()

    offset = lax.axis_index("win") * row_count
    pick_at = lax.broadcasted_iota(jnp.int32, (2 * row_count, 2 * BLOCK), 0)
    pick_lane = lax.broadcasted_iota(jnp.int32, (2 * row_count, 2 * BLOCK), 1)
    want = pick_at % row_count + offset + pick_at // row_count * BLOCK
    pick = (pick_lane == want).astype(jnp.bfloat16)
    turn_at = lax.broadcasted_iota(jnp.int32, (depth, depth), 0)
    turn_lane = lax.broadcasted_iota(jnp.int32, (depth, depth), 1)
    turn = jnp.where(
        turn_at % 2 == 1,
        jnp.where(turn_lane == turn_at - 1, -1.0, 0.0),
        jnp.where(turn_lane == turn_at + 1, 1.0, 0.0),
    ).astype(jnp.bfloat16)
    place = lax.broadcasted_iota(jnp.int32, (2 * row_count, width), 1) // depth

    def prepare(halves, first, at):
        near = pl.ds(pl.multiple_of((at - first) * 2 * BLOCK, 2 * BLOCK), 2 * BLOCK)
        here = pl.ds(pl.multiple_of(at * 2 * BLOCK, 2 * BLOCK), 2 * BLOCK)
        pieces = [ref[:, here] for ref in whole] + [ref[:, near] for ref in halves]
        rows = jnp.concatenate(pieces, axis=0)
        turned = jnp.dot(turn, rows, preferred_element_type=jnp.float32).astype(jnp.bfloat16)
        left = lax.dot_general(
            pick,
            jnp.concatenate([rows] * copies, axis=0),
            (((1,), (1,)), ((), ())),
            preferred_element_type=jnp.float32,
        )
        where = pl.multiple_of(at * 2 * row_count, 2 * row_count)
        for copy in range(copies):
            only = left if copies == 1 else jnp.where(place == copy, left, 0.0)
            left_ref[copy, pl.ds(where, 2 * row_count), :] = only.astype(jnp.bfloat16)
        for half in range(2):
            lanes = slice(half * BLOCK, (half + 1) * BLOCK)
            right_ref[at * 2 + half, :, :BLOCK] = rows[:, lanes]
            right_ref[at * 2 + half, :, BLOCK:] = turned[:, lanes]

    pairs = whole[0].shape[1] // (2 * BLOCK)
    span = math.gcd(pairs // 2, 8)
    parts = pairs // span

    def prepare_to(done, need):
        def part(halves, first, at, carry):
            for pair in range(span):
                prepare(halves, first, at * span + pair)
            return carry

        if not half_count:
            lax.fori_loop(done, need, functools.partial(part, [], 0), 0)
            return
        middle = parts // 2
        lax.fori_loop(done, jnp.minimum(need, middle), functools.partial(part, lows, 0), 0)
        first = functools.partial(part, highs, middle * span)
        lax.fori_loop(jnp.maximum(done, middle), need, first, 0)

    prepare_to(0, 1)
    lists.wait()

    def send(first, slot, tiles_here):
        for tile in tiles_here:
            to = lists_ref[2 * total + first + tile]
            pltpu.make_async_copy(
                ring_ref.at[slot, tile], out_ref.at[to, freq], sems.at[slot]
            ).start()

    def sent(slot, count):
        pltpu.make_async_copy(
            ring_ref.at[slot, pl.ds(0, count)], out_ref.at[pl.ds(0, count), freq], sems.at[slot]
        ).wait()

    def compute(first, slot, count):
        for group in range(count // pack):
            lefts = []
            rights = []
            for member in range(pack):
                at = first + group * pack + member
                left_at = pl.multiple_of(lists_ref[at] * row_count, row_count)
                left = left_ref[member % copies, pl.ds(left_at, row_count), :]
                if chunks > 1:
                    chunk = member // copies
                    empty = jnp.zeros_like(left)
                    left = jnp.concatenate(
                        [left if spot == chunk else empty for spot in range(chunks)], axis=1
                    )
                lefts.append(left)
                rights.append(right_ref[lists_ref[total + at]])
            product = jnp.dot(
                jnp.concatenate(lefts, axis=0),
                jnp.concatenate(rights, axis=0),
                preferred_element_type=jnp.float32,
            )
            product = product * scale
            for member in range(pack):
                mine = product[member * row_count : (member + 1) * row_count]
                ring_ref[slot, group * pack + member, 0] = mine[:, :BLOCK]
                ring_ref[slot, group * pack + member, 1] = mine[:, BLOCK:]

    def needed(last):
        return lists_ref[total + last] // (2 * span) + 1

    steps = total // tiles
    rest = total % tiles

    def stack(step, done):
        first = step * tiles
        slot = lax.rem(step, slots)
        need = jnp.maximum(needed(first + tiles - 1), done)
        prepare_to(done, need)

        @pl.when(step >= slots)
        def _():
            sent(slot, tiles)

        compute(first, slot, tiles)
        send(first, slot, range(tiles))
        return need

    done = lax.fori_loop(0, steps, stack, jnp.int32(1))
    flying = [(step % slots, tiles) for step in range(steps)][-slots:]
    if rest:
        prepare_to(done, needed(total - 1))
        slot = steps % slots
        if steps >= slots:
            sent(slot, tiles)
            flying = flying[1:]
        compute(steps * tiles, slot, rest)
        send(steps * tiles, slot, range(rest))
        flying.append((slot, rest))
    for slot, count in flying:
        sent(slot, count)


def stack_bin(freq, out_shape, lists, whole, lows, highs, scale, so_far):
    pieces = whole + lows + highs
    channels = whole[0].shape[1]
    depth = sum(value.shape[0] for value in whole + lows)
    tile_total, _, parts, row_count, _ = out_shape.shape
    pack = math.gcd(tile_total, max(1, MXU // depth))
    copies = min(pack, max(1, BLOCK // depth))
    tiles = max(pack, 36 // pack * pack)
    tiles = min(tiles, tile_total)
    blocks = channels // BLOCK
    vmem = pl.BlockSpec(memory_space=pltpu.VMEM)
    in_specs = [pl.BlockSpec(memory_space=pl.ANY)] + [vmem] * len(pieces)
    operands = [lists] + pieces
    aliases = {}
    if so_far is not None:
        in_specs.append(pl.BlockSpec(memory_space=pl.ANY))
        aliases = {len(operands): 0}
        operands.append(so_far)
    slots = 4
    scratch = [
        ((copies, blocks * row_count, copies * depth), jnp.bfloat16),
        ((blocks, depth, 2 * BLOCK), jnp.bfloat16),
        ((slots, tiles, parts, row_count, BLOCK), jnp.float32),
    ]
    used = [(value.shape, value.dtype) for value in pieces] + scratch
    vmem_bytes = sum(math.prod(shape) * jnp.dtype(kind).itemsize for shape, kind in used)
    return pl.pallas_call(
        functools.partial(stack_kernel, (len(whole), len(lows), len(aliases)), freq, scale, pack),
        out_shape=out_shape,
        in_specs=in_specs,
        out_specs=pl.BlockSpec(memory_space=pl.ANY),
        scratch_shapes=[pltpu.VMEM(*spec) for spec in scratch]
        + [pltpu.SMEM(lists.shape, jnp.int32)]
        + [pltpu.SemaphoreType.DMA((slots,)), pltpu.SemaphoreType.DMA],
        input_output_aliases=aliases,
        cost_estimate=pl.CostEstimate(flops=0, bytes_accessed=0, transcendentals=0),
        compiler_params=pltpu.CompilerParams(vmem_limit_bytes=vmem_bytes + 8 * 1024 * 1024),
        name="stack",
    )(*operands)


def on_device(spectra, tile_rows, tile_cols):
    window_total = spectra.shape[2] * math.prod(
        lax.axis_size(axis) for axis in ("chip", "core", "col", "win")
    )
    scale = float(1.0 / window_total**0.5)
    freqs = spectra.shape[1]
    row_count = BLOCK // lax.axis_size("win")
    out_shape = jax.ShapeDtypeStruct(
        (tile_rows.shape[0], freqs, 2, row_count, BLOCK), jnp.float32
    )
    lists = by_column(tile_rows, tile_cols)
    slabs = whiten(spectra[0])
    block = gather_line(slabs[0])
    block, lists = lax.optimization_barrier((block, lists))
    swapped = swap_cores([block])
    arrived, lows, highs = gather_relayed(block)
    near, far = arrived, lows + highs
    whole = [block] + swapped + arrived + swap_cores(arrived)
    lows = lows + swap_cores(lows)
    highs = highs + swap_cores(highs)
    later = []
    for own in slabs[1:]:
        block = gather_line(after(own, *swapped))
        swapped = swap_cores([block])
        arrived = gather_direct(block, near, far)
        near, far = arrived, arrived
        later.append(([block] + swapped, arrived))
    out = stack_bin(0, out_shape, lists, whole, lows, highs, scale, None)
    for freq, (whole, arrived) in enumerate(later, 1):
        arrived = list(after(tuple(arrived), out))
        whole = whole + arrived + swap_cores(arrived)
        out = stack_bin(freq, out_shape, lists, whole, [], [], scale, out)
    return out


def solution(mesh):
    rows, cols, wins = (mesh.shape[axis] for axis in ("row", "col", "win"))
    cores = 2 if rows % 2 == 0 else 1
    mesh = jax.sharding.Mesh(
        mesh.devices.reshape(rows // cores, cores, cols, wins), ("chip", "core", "col", "win")
    )
    devices = ("chip", "core", "col")
    in_specs = (P("win", None, devices, None, None), P(devices), P(devices))
    out_specs = P(devices, None, None, "win", None)
    return jax.shard_map(
        on_device, mesh=mesh, in_specs=in_specs, out_specs=out_specs, check_vma=False
    )
```

```python
import functools
import math

import jax
import jax.numpy as jnp
from jax import lax
from jax.experimental import pallas as pl
from jax.experimental.pallas import tpu as pltpu
from jax.sharding import PartitionSpec as P

BLOCK = 128
MXU = 256
LAG = 3


def whiten_kernel(spectra_ref, *out_refs):
    freqs = spectra_ref.shape[0]
    power = None
    for freq in range(freqs):
        for part in range(2):
            row = spectra_ref[freq, :, part : part + 1, :]
            power = row * row if power is None else power + row * row
    factor = jnp.minimum(lax.rsqrt(power / freqs), 1.0)
    for freq in range(freqs):
        out_refs[freq][...] = (spectra_ref[freq] * factor).astype(jnp.bfloat16)


def whiten(spectra):
    freqs, windows, parts, channels = spectra.shape
    shape = jax.ShapeDtypeStruct((windows, parts, channels), jnp.bfloat16)
    slabs = pl.pallas_call(whiten_kernel, out_shape=[shape] * freqs, name="whiten")(spectra)
    return [slab.reshape(windows * parts, channels) for slab in slabs]


def after(value, *earlier):
    return lax.optimization_barrier((value, *earlier))[0]


def shift(value, axis, step):
    size = lax.axis_size(axis)
    return lax.ppermute(value, axis, [(at, (at + step) % size) for at in range(size)])


def gather_line(own):
    line = [own] + [shift(own, "col", step) for step in range(1, lax.axis_size("col"))]
    return jnp.concatenate(line, axis=0)


def gather_direct(block, near, far):
    chips, wins = lax.axis_size("chip"), lax.axis_size("win")
    blocks = []
    for step in range(1, chips * wins):
        chip_step, win_step = step % chips, step // chips
        perm = []
        for chip in range(chips):
            for win in range(wins):
                to = (chip + chip_step) % chips * wins + (win + win_step) % wins
                perm.append((chip * wins + win, to))
        sent = after(block, *(far if chip_step and win_step else near))
        blocks.append(lax.ppermute(sent, ("chip", "win"), perm))
    return blocks


def by_column(tile_rows, tile_cols):
    total = tile_rows.shape[0]
    place = jnp.arange(total, dtype=jnp.int32)
    key = tile_cols * total + place
    rank = jnp.sum((key[None, :] < key[:, None]).astype(jnp.int32), axis=1)
    hit = rank[None, :] == place[:, None]
    return jnp.concatenate(
        [
            jnp.sum(jnp.where(hit, values[None, :], 0), axis=1)
            for values in (tile_rows, tile_cols, place)
        ]
    )


def gather_relayed(block):
    half = block.shape[1] // 2
    along_chip = [shift(block, "chip", step) for step in range(1, lax.axis_size("chip"))]
    along_win = [shift(block, "win", step) for step in range(1, lax.axis_size("win"))]
    lows = []
    highs = []
    for chip_step, from_chip in enumerate(along_chip, 1):
        for win_step, from_win in enumerate(along_win, 1):
            lows.append(shift(from_win[:, :half], "chip", chip_step))
            highs.append(shift(from_chip[:, half:], "win", win_step))
    return along_chip + along_win, lows, highs


def swap_cores(values):
    return [shift(value, "core", 1) for value in values] if lax.axis_size("core") == 2 else []


def stack_kernel(counts, freq, scale, pack, lists_hbm, *refs):
    whole_count, half_count, aliased = counts
    whole = refs[:whole_count]
    lows = refs[whole_count : whole_count + half_count]
    piece_count = whole_count + 2 * half_count
    highs = refs[whole_count + half_count : piece_count]
    out_ref, left_ref, right_ref, ring_ref, lists_ref, sems, list_sem = refs[
        piece_count + aliased :
    ]
    total = out_ref.shape[0]
    copies, _, width = left_ref.shape
    depth = right_ref.shape[1]
    slots, tiles, _, row_count, _ = ring_ref.shape
    chunks = pack // copies

    lists = pltpu.make_async_copy(lists_hbm, lists_ref, list_sem)
    lists.start()

    offset = lax.axis_index("win") * row_count
    pick_at = lax.broadcasted_iota(jnp.int32, (2 * row_count, 2 * BLOCK), 0)
    pick_lane = lax.broadcasted_iota(jnp.int32, (2 * row_count, 2 * BLOCK), 1)
    want = pick_at % row_count + offset + pick_at // row_count * BLOCK
    pick = (pick_lane == want).astype(jnp.bfloat16)
    turn_at = lax.broadcasted_iota(jnp.int32, (depth, depth), 0)
    turn_lane = lax.broadcasted_iota(jnp.int32, (depth, depth), 1)
    turn = jnp.where(
        turn_at % 2 == 1,
        jnp.where(turn_lane == turn_at - 1, -1.0, 0.0),
        jnp.where(turn_lane == turn_at + 1, 1.0, 0.0),
    ).astype(jnp.bfloat16)
    place = lax.broadcasted_iota(jnp.int32, (2 * row_count, width), 1) // depth

    def prepare(halves, first, at):
        near = pl.ds(pl.multiple_of((at - first) * 2 * BLOCK, 2 * BLOCK), 2 * BLOCK)
        here = pl.ds(pl.multiple_of(at * 2 * BLOCK, 2 * BLOCK), 2 * BLOCK)
        pieces = [ref[:, here] for ref in whole] + [ref[:, near] for ref in halves]
        rows = jnp.concatenate(pieces, axis=0)
        turned = jnp.dot(turn, rows, preferred_element_type=jnp.float32).astype(jnp.bfloat16)
        left = lax.dot_general(
            pick,
            jnp.concatenate([rows] * copies, axis=0),
            (((1,), (1,)), ((), ())),
            preferred_element_type=jnp.float32,
        )
        where = pl.multiple_of(at * 2 * row_count, 2 * row_count)
        for copy in range(copies):
            only = left if copies == 1 else jnp.where(place == copy, left, 0.0)
            left_ref[copy, pl.ds(where, 2 * row_count), :] = only.astype(jnp.bfloat16)
        for half in range(2):
            lanes = slice(half * BLOCK, (half + 1) * BLOCK)
            right_ref[at * 2 + half, :, :BLOCK] = rows[:, lanes]
            right_ref[at * 2 + half, :, BLOCK:] = turned[:, lanes]

    pairs = whole[0].shape[1] // (2 * BLOCK)
    span = math.gcd(pairs // 2, 8)
    parts = pairs // span

    def prepare_to(done, need):
        def part(halves, first, at, carry):
            for pair in range(span):
                prepare(halves, first, at * span + pair)
            return carry

        if not half_count:
            lax.fori_loop(done, need, functools.partial(part, [], 0), 0)
            return
        middle = parts // 2
        lax.fori_loop(done, jnp.minimum(need, middle), functools.partial(part, lows, 0), 0)
        first = functools.partial(part, highs, middle * span)
        lax.fori_loop(jnp.maximum(done, middle), need, first, 0)

    prepare_to(0, 1)
    lists.wait()

    def send(first, slot, tiles_here):
        for tile in tiles_here:
            to = lists_ref[2 * total + first + tile]
            pltpu.make_async_copy(
                ring_ref.at[slot, tile], out_ref.at[to, freq], sems.at[slot]
            ).start()

    def sent(slot, count):
        pltpu.make_async_copy(
            ring_ref.at[slot, pl.ds(0, count)], out_ref.at[pl.ds(0, count), freq], sems.at[slot]
        ).wait()

    def compute(first, slot, count):
        for group in range(count // pack):
            lefts = []
            rights = []
            for member in range(pack):
                at = first + group * pack + member
                left_at = pl.multiple_of(lists_ref[at] * row_count, row_count)
                left = left_ref[member % copies, pl.ds(left_at, row_count), :]
                if chunks > 1:
                    chunk = member // copies
                    empty = jnp.zeros_like(left)
                    left = jnp.concatenate(
                        [left if spot == chunk else empty for spot in range(chunks)], axis=1
                    )
                lefts.append(left)
                rights.append(right_ref[lists_ref[total + at]])
            product = jnp.dot(
                jnp.concatenate(lefts, axis=0),
                jnp.concatenate(rights, axis=0),
                preferred_element_type=jnp.float32,
            )
            product = product * scale
            for member in range(pack):
                mine = product[member * row_count : (member + 1) * row_count]
                ring_ref[slot, group * pack + member, 0] = mine[:, :BLOCK]
                ring_ref[slot, group * pack + member, 1] = mine[:, BLOCK:]
            ready = (group + 1 - LAG) * pack
            send(first, slot, range(max(0, ready - pack), max(0, ready)))
        send(first, slot, range(max(0, count - LAG * pack), count))

    def needed(last):
        return lists_ref[total + last] // (2 * span) + 1

    steps = total // tiles
    rest = total % tiles

    def stack(step, done):
        first = step * tiles
        slot = lax.rem(step, slots)
        need = jnp.maximum(needed(first + tiles - 1), done)
        prepare_to(done, need)

        @pl.when(step >= slots)
        def _():
            sent(slot, tiles)

        compute(first, slot, tiles)
        return need

    done = lax.fori_loop(0, steps, stack, jnp.int32(1))
    flying = [(step % slots, tiles) for step in range(steps)][-slots:]
    if rest:
        prepare_to(done, needed(total - 1))
        slot = steps % slots
        if steps >= slots:
            sent(slot, tiles)
            flying = flying[1:]
        compute(steps * tiles, slot, rest)
        flying.append((slot, rest))
    for slot, count in flying:
        sent(slot, count)


def stack_bin(freq, out_shape, lists, whole, lows, highs, scale, so_far):
    pieces = whole + lows + highs
    channels = whole[0].shape[1]
    depth = sum(value.shape[0] for value in whole + lows)
    tile_total, _, parts, row_count, _ = out_shape.shape
    pack = math.gcd(tile_total, max(1, MXU // depth))
    copies = min(pack, max(1, BLOCK // depth))
    tiles = max(pack, 72 // pack * pack)
    tiles = min(tiles, tile_total)
    blocks = channels // BLOCK
    vmem = pl.BlockSpec(memory_space=pltpu.VMEM)
    in_specs = [pl.BlockSpec(memory_space=pl.ANY)] + [vmem] * len(pieces)
    operands = [lists] + pieces
    aliases = {}
    if so_far is not None:
        in_specs.append(pl.BlockSpec(memory_space=pl.ANY))
        aliases = {len(operands): 0}
        operands.append(so_far)
    slots = 3
    scratch = [
        ((copies, blocks * row_count, copies * depth), jnp.bfloat16),
        ((blocks, depth, 2 * BLOCK), jnp.bfloat16),
        ((slots, tiles, parts, row_count, BLOCK), jnp.float32),
    ]
    used = [(value.shape, value.dtype) for value in pieces] + scratch
    vmem_bytes = sum(math.prod(shape) * jnp.dtype(kind).itemsize for shape, kind in used)
    return pl.pallas_call(
        functools.partial(stack_kernel, (len(whole), len(lows), len(aliases)), freq, scale, pack),
        out_shape=out_shape,
        in_specs=in_specs,
        out_specs=pl.BlockSpec(memory_space=pl.ANY),
        scratch_shapes=[pltpu.VMEM(*spec) for spec in scratch]
        + [pltpu.SMEM(lists.shape, jnp.int32)]
        + [pltpu.SemaphoreType.DMA((slots,)), pltpu.SemaphoreType.DMA],
        input_output_aliases=aliases,
        cost_estimate=pl.CostEstimate(flops=0, bytes_accessed=0, transcendentals=0),
        compiler_params=pltpu.CompilerParams(vmem_limit_bytes=vmem_bytes + 8 * 1024 * 1024),
        name="stack",
    )(*operands)


def on_device(spectra, tile_rows, tile_cols):
    window_total = spectra.shape[2] * math.prod(
        lax.axis_size(axis) for axis in ("chip", "core", "col", "win")
    )
    scale = float(1.0 / window_total**0.5)
    freqs = spectra.shape[1]
    row_count = BLOCK // lax.axis_size("win")
    out_shape = jax.ShapeDtypeStruct(
        (tile_rows.shape[0], freqs, 2, row_count, BLOCK), jnp.float32
    )
    lists = by_column(tile_rows, tile_cols)
    slabs = whiten(spectra[0])
    block = gather_line(slabs[0])
    block, lists = lax.optimization_barrier((block, lists))
    swapped = swap_cores([block])
    arrived, lows, highs = gather_relayed(block)
    near, far = arrived, lows + highs
    whole = [block] + swapped + arrived + swap_cores(arrived)
    lows = lows + swap_cores(lows)
    highs = highs + swap_cores(highs)
    later = []
    for own in slabs[1:]:
        block = gather_line(after(own, *swapped))
        swapped = swap_cores([block])
        arrived = gather_direct(block, near, far)
        near, far = arrived, arrived
        later.append(([block] + swapped, arrived))
    out = stack_bin(0, out_shape, lists, whole, lows, highs, scale, None)
    for freq, (whole, arrived) in enumerate(later, 1):
        arrived = list(after(tuple(arrived), out))
        whole = whole + arrived + swap_cores(arrived)
        out = stack_bin(freq, out_shape, lists, whole, [], [], scale, out)
    return out


def solution(mesh):
    rows, cols, wins = (mesh.shape[axis] for axis in ("row", "col", "win"))
    cores = 2 if rows % 2 == 0 else 1
    mesh = jax.sharding.Mesh(
        mesh.devices.reshape(rows // cores, cores, cols, wins), ("chip", "core", "col", "win")
    )
    devices = ("chip", "core", "col")
    in_specs = (P("win", None, devices, None, None), P(devices), P(devices))
    out_specs = P(devices, None, None, "win", None)
    return jax.shard_map(
        on_device, mesh=mesh, in_specs=in_specs, out_specs=out_specs, check_vma=False
    )
```
